512 devices in a mesh: patch: 2 (over core), lat: 64 (over z, y), rad: 4 (over x).
Axes of the slice: x: 4, y: 4, z: 16, core: 2. Of those that a mesh axis runs over, the one named last changes fastest.
Arguments:
- iterate_in: float32 [2, 4, 8, 1024, 256], P('patch', None, 'rad', 'lat'), may hold values from -6 to 6
- forcing: float32 [2, 4, 8, 1024, 256], P('patch', None, 'rad', 'lat'), may hold values from -6 to 6
- viscosity: float32 [2, 8, 1024, 256], P('patch', 'rad', 'lat'), may hold values from 0.1 to 10
- vanka_inverse: float32 [2, 4, 4, 8, 1024, 256], P('patch', None, None, 'rad', 'lat'), may hold values from -1 to 2, as said below
- pack_cells: int32 [2, 64, 64, 4], P('patch', 'lat'), may hold values from 0 to 4095
- take_slot: int32 [2, 64, 32, 4], P('patch', 'lat'), may hold values from 0 to 255, as said below
- take_weight: float32 [2, 64, 32, 4], P('patch', 'lat'), may hold values from 0.1 to 0.4
Outputs:
- iterate: float32 [2, 4, 8, 1024, 256], P('patch', None, 'rad', 'lat')
- coarse_correction: float32 [2, 4, 4, 512, 128], P('patch', None, 'rad', 'lat')
The draws below stay inside these ranges and needn't reach their ends.
Inputs may be any that keep to these rules, and one draw needn't show every extreme that they name: `take_slot`: A slot s names source strip s // 4, which lies among the 32 strips starting at the destination strip minus 32 // 2, cyclically. `vanka_inverse`: symmetric per cell.
All inputs are finite; a program needn't handle non-finite values.
Results may differ from the reference program's by a relative error of at most 0.0001.
Values sent between devices are 32-bit elements; how exact they have to be, the bound alone decides.
A program may use at most 64 MiB of HBM per device.

```python
import math
import jax
import jax.numpy as jnp

CB = 16
NA = 256
CAP = 4
SWEEPS = 3
NR = 8
NPHI = 1024
WIN = 32
N_LAT = 64


def viscosity_field(key):
    exponent = jax.random.uniform(key, (2, NR, NPHI, NA), jnp.float32, -1.0, 1.0)
    return jnp.exp(exponent * math.log(10.0))


def draw_viscosity(key, part):
    shared = viscosity_field(key)
    return shared


def draw_vanka_inverse(key, part):
    viscous = viscosity_field(key)
    key = jax.random.fold_in(key, 5)
    padded = jnp.pad(viscous, ((0, 0), (1, 1), (1, 1), (1, 1)), mode='edge')
    faces = jnp.zeros_like(viscous)
    for spatial in range(3):
        for offset in (1, -1):
            picks = [slice(1, -1), slice(1, -1), slice(1, -1)]
            picks[spatial] = slice(2, None) if offset > 0 else slice(0, -2)
            faces = faces + 0.5 * (viscous + padded[(slice(None),) + tuple(picks)])
    scales = jnp.stack([faces, faces, faces, 6.0 / viscous], axis=1)
    noise = jax.random.uniform(key, (2, 4, 4, NR, NPHI, NA), jnp.float32, -1.0, 1.0)
    symmetric = 0.5 * (noise + jnp.swapaxes(noise, 1, 2))
    identity = jnp.eye(4, dtype=jnp.float32)[None, :, :, None, None, None]
    block = identity + 0.3 * symmetric * (1.0 - identity)
    root = 1.0 / jnp.sqrt(scales)
    return block * root[:, :, None] * root[:, None, :]


def draw_take_slot(key, part):
    key = jax.random.fold_in(key, 11)
    first_key, second_key = jax.random.split(key)
    offsets = jax.random.randint(first_key, (2, N_LAT, 2 * CB, 4), 0, WIN)
    places = jax.random.randint(second_key, (2, N_LAT, 2 * CB, 4), 0, CAP)
    target = jnp.arange(N_LAT, dtype=jnp.int32)[None, :, None, None]
    strips = (target + offsets - WIN // 2 + N_LAT) % N_LAT
    return (strips * CAP + places).astype(jnp.int32)


def with_ends(values, rng, least, largest):
    shape = values.shape
    spot = [jax.random.randint(jax.random.fold_in(rng, axis), (), 0, shape[axis]) for axis in range(len(shape))]
    values = values.at[tuple(spot)].set(least)
    longest = shape.index(max(shape))
    spot[longest] = (spot[longest] + 1) % shape[longest]
    return values.at[tuple(spot)].set(largest)


def levels(rng, extent, cuts, low, high):
    def one(dim, blocks):
        heights = jax.random.uniform(jax.random.fold_in(jax.random.fold_in(rng, 6), dim), (blocks,), jnp.float32, low / len(cuts), high / len(cuts))
        return jnp.repeat(jnp.exp(heights), extent[dim] // blocks).reshape((-1,) + (1,) * (len(extent) - dim - 1))

    loudness = one(*cuts[0])
    for cut in cuts[1:]:
        loudness = loudness * one(*cut)
    return loudness


def centred(own_key, dims, deviation, most, cuts=(), kind=jnp.bfloat16):
    values = deviation * jax.random.normal(own_key, dims, jnp.float32)
    if cuts:
        values = values * levels(own_key, dims, cuts, -0.22, 0.18)
    return jnp.clip(values, -most, most).astype(kind)


def setup_inputs(seed: int = 0) -> dict:
    arg_keys = jax.random.split(jax.random.key(seed), 8)
    return {
        "iterate_in": centred(arg_keys[0], (2, 4, NR, NPHI, NA), 1.0, 6.0, ((0, 2), (2, 4), (3, 64)), jnp.float32),
        "forcing": centred(arg_keys[1], (2, 4, NR, NPHI, NA), 1.0, 6.0, ((0, 2), (2, 4), (3, 64)), jnp.float32),
        "viscosity": draw_viscosity(jax.random.fold_in(arg_keys[7], 71), 0),
        "vanka_inverse": draw_vanka_inverse(jax.random.fold_in(arg_keys[7], 71), 0),
        "pack_cells": with_ends(jax.random.randint(arg_keys[4], (2, N_LAT, N_LAT, CAP), 0, CB * NA), jax.random.fold_in(arg_keys[4], 1), 0, (CB * NA) - 1).astype(jnp.int32),
        "take_slot": draw_take_slot(jax.random.fold_in(arg_keys[7], 71), 0),
        "take_weight": jnp.clip(0.1 + 0.3 * jax.random.uniform(arg_keys[6], (2, N_LAT, 2 * CB, 4), jnp.float32) ** levels(arg_keys[6], (2, N_LAT, 2 * CB, 4), ((0, 2), (1, 64)), -0.2, 0.2), 0.1, 0.4),
    }


OMEGA = 0.8


def interior(array, spatial, offset):
    picks = [slice(1, -1), slice(1, -1), slice(1, -1)]
    picks[spatial] = slice(2, None) if offset > 0 else slice(0, -2)
    leading = (slice(None),) * (array.ndim - 3)
    return array[leading + tuple(picks)]


def operate(padded, viscous, lap_scale, grad_scale):
    centre = padded[:, 1:-1, 1:-1, 1:-1]
    middle = viscous[1:-1, 1:-1, 1:-1]
    friction = jnp.zeros_like(centre[:3])
    pressure_sum = jnp.zeros_like(middle)
    divergence = jnp.zeros_like(middle)
    gradients = []
    for spatial in range(3):
        upper_cell = interior(padded, spatial, 1)
        lower_cell = interior(padded, spatial, -1)
        upper_face = 0.5 * (middle + interior(viscous, spatial, 1))
        lower_face = 0.5 * (middle + interior(viscous, spatial, -1))
        friction = friction + upper_face * (centre[:3] - upper_cell[:3]) + lower_face * (centre[:3] - lower_cell[:3])
        pressure_sum = pressure_sum + upper_cell[3] + lower_cell[3]
        gradients.append(0.5 * (upper_cell[3] - lower_cell[3]))
        divergence = divergence + 0.5 * (upper_cell[spatial] - lower_cell[spatial])
    velocity = lap_scale * friction + grad_scale * jnp.stack(gradients)
    pressure = lap_scale * (6.0 * centre[3] - pressure_sum) / middle - grad_scale * divergence
    return jnp.concatenate([velocity, pressure[None]], axis=0)


def diagonal(viscous, lap_scale):
    middle = viscous[1:-1, 1:-1, 1:-1]
    faces = jnp.zeros_like(middle)
    for spatial in range(3):
        for offset in (1, -1):
            faces = faces + 0.5 * (middle + interior(viscous, spatial, offset))
    return lap_scale * jnp.stack([faces, faces, faces, 6.0 / middle])


def restrict(field):
    shape = field.shape
    lead = shape[:-3]
    blocks = field.reshape(lead + (shape[-3] // 2, 2, shape[-2] // 2, 2, shape[-1] // 2, 2))
    count = len(lead)
    return jnp.mean(blocks, axis=(count + 1, count + 3, count + 5))


def edge_latitude(padded):
    return jnp.pad(padded, ((0, 0), (0, 0), (1, 1)), mode="edge")


def rim_values(source, pack_cells, take_slot, take_weight, patch):
    slots = take_slot[patch]
    strips = slots // CAP
    places = slots % CAP
    target = jnp.arange(N_LAT, dtype=jnp.int32)[:, None, None]
    cells = pack_cells[1 - patch][strips, target, places]
    columns = strips * CB + cells // NA
    latitudes = cells % NA
    values = source[:, :, columns, latitudes]
    ghosts = jnp.sum(values * take_weight[patch], axis=-1)
    lower = ghosts[..., :CB].reshape(4, NR, NPHI)
    upper = ghosts[..., CB:].reshape(4, NR, NPHI)
    return lower, upper


def pad_iterate(field, lower, upper):
    middle = jnp.pad(field, ((0, 0), (1, 1), (1, 1), (0, 0)))
    lower_pad = jnp.pad(lower, ((0, 0), (1, 1), (1, 1)))[..., None]
    upper_pad = jnp.pad(upper, ((0, 0), (1, 1), (1, 1)))[..., None]
    return jnp.concatenate([lower_pad, middle, upper_pad], axis=3)


def reference(iterate_in, forcing, viscosity, vanka_inverse, pack_cells, take_slot, take_weight):
    viscous = [edge_latitude(jnp.pad(viscosity[patch], ((1, 1), (1, 1), (0, 0)))) for patch in range(2)]

    def residual_of(current):
        results = []
        for patch in range(2):
            lower, upper = rim_values(current[1 - patch], pack_cells, take_slot, take_weight, patch)
            padded = pad_iterate(current[patch], lower, upper)
            results.append(forcing[patch] - operate(padded, viscous[patch], 1.0, 1.0))
        return jnp.stack(results)

    iterate = iterate_in
    for sweep in range(SWEEPS):
        residual = residual_of(iterate)
        iterate = iterate + OMEGA * jnp.sum(vanka_inverse * residual[:, None], axis=2)
    coarse_residual = restrict(residual_of(iterate))
    coarse_eta = restrict(viscosity)
    corrections = []
    for patch in range(2):
        coarse_visc = edge_latitude(jnp.pad(coarse_eta[patch], ((1, 1), (1, 1), (0, 0))))
        scaling = diagonal(coarse_visc, 0.25)
        first = OMEGA * coarse_residual[patch] / scaling
        padded = jnp.pad(first, ((0, 0), (1, 1), (1, 1), (1, 1)))
        second = first + OMEGA * (coarse_residual[patch] - operate(padded, coarse_visc, 0.25, 0.5)) / scaling
        corrections.append(second)
    return iterate, jnp.stack(corrections)
```

```python
import functools

import jax
import jax.numpy as jnp
from jax import lax
from jax.experimental import pallas as pl
from jax.experimental.pallas import tpu as pltpu
from jax.sharding import PartitionSpec as P

SWEEPS = 3
OMEGA = 0.8
WIN = 32
CAP = 4
RIM, RAD, PHI, ETA_RAD, COARSE_RAD, ETA_PHI, FIRST_RAD, FIRST_PHI = 0, 4, 12, 20, 22, 24, 26, 28
F32 = jnp.float32


def exact_dot(values, zero_one):
    high = values.astype(jnp.bfloat16)
    rest = values - high.astype(F32)
    middle = rest.astype(jnp.bfloat16)
    low = (rest - middle.astype(F32)).astype(jnp.bfloat16)
    dot = functools.partial(jnp.dot, preferred_element_type=F32)
    return dot(high, zero_one) + (dot(middle, zero_one) + dot(low, zero_one))


def kernel(
    strips, layers,
    iterate_hbm, forcing_hbm, eta_hbm, inverse_hbm, cells_hbm, slots_hbm, weights_hbm,
    iterate_out, coarse_out,
    cur, frc, eta, vin, cel, slt, wgt,
    onehot, pick, pick_edge, weigh, diag, w_phi, w_lat, w_rad, inv_eta, gain, edge_w, edge_ie,
    rim_send, rim_recv, rad_recv, phi_send, phi_recv,
    eta_rad, eta_phi_send, eta_phi, ceta, ceta_rad, cdia, cfaces,
    first, first_rad, first_phi_send, first_phi, fold,
    local_sem, send_sem, recv_sem,
):
    patch, lat, rad = lax.axis_index("patch"), lax.axis_index("lat"), lax.axis_index("rad")
    _, _, width, na = frc.shape
    half = na // 2
    below = (patch, lat, lax.rem(rad + layers - 1, layers))
    above = (patch, lat, lax.rem(rad + 1, layers))
    left = (patch, lax.rem(lat + strips - 1, strips), rad)
    right = (patch, lax.rem(lat + 1, strips), rad)
    has_below, has_above = rad > 0, rad < layers - 1
    has_left, has_right = lat > 0, lat < strips - 1

    def across(offset):
        return (1 - patch, lax.rem(lat + offset + strips, strips), rad)

    loads = [
        pltpu.make_async_copy(iterate_hbm, cur.at[0], local_sem.at[0]),
        pltpu.make_async_copy(cells_hbm, cel.at[pl.ds(0, strips)], local_sem.at[1]),
        pltpu.make_async_copy(cells_hbm, cel.at[pl.ds(strips, strips)], local_sem.at[2]),
        pltpu.make_async_copy(eta_hbm, eta, local_sem.at[3]),
        pltpu.make_async_copy(slots_hbm, slt, local_sem.at[4]),
        pltpu.make_async_copy(weights_hbm, wgt, local_sem.at[5]),
        pltpu.make_async_copy(forcing_hbm, frc, local_sem.at[6]),
    ]
    for i in range(4):
        loads.append(
            pltpu.make_async_copy(
                inverse_hbm.at[i, pl.ds(i, 4 - i)], vin.at[i, pl.ds(i, 4 - i)], local_sem.at[7 + i]
            )
        )
    for load in loads:
        load.start()

    barrier = pltpu.get_barrier_semaphore()

    def greet(device):
        pl.semaphore_signal(barrier, inc=1, device_id=device, device_id_type=pl.DeviceIdType.MESH)

    for offset in sorted(range(-WIN // 2, WIN // 2), key=lambda o: -abs(o)):
        greet(across(offset))
    for device in (below, above, left, right):
        greet(device)

    def remote(src, dst, sem, device):
        return pltpu.make_async_remote_copy(
            src_ref=src, dst_ref=dst, send_sem=send_sem.at[sem], recv_sem=recv_sem.at[sem],
            device_id=device, device_id_type=pl.DeviceIdType.MESH,
        )

    def rad_copies(k):
        return [
            remote(cur.at[k, :, 1], rad_recv.at[k, 0], RAD + 2 * k, above),
            remote(cur.at[k, :, 0], rad_recv.at[k, 1], RAD + 2 * k + 1, below),
        ]

    def phi_copies(k):
        return [
            remote(phi_send.at[k, 0], phi_recv.at[k, 0], PHI + 2 * k, right),
            remote(phi_send.at[k, 1], phi_recv.at[k, 1], PHI + 2 * k + 1, left),
        ]

    def rim_start(k):
        for slot in sorted(range(WIN), key=lambda s: -abs(s - WIN // 2 + 1)):
            remote(
                rim_send.at[k, pl.ds(slot, 1)], rim_recv.at[k, pl.ds(WIN - 1 - slot, 1)], RIM + k,
                across(slot - WIN // 2 + 1),
            ).start()

    def rim_all(k, sem):
        return pltpu.make_async_copy(rim_recv.at[k], rim_recv.at[k], sem.at[RIM + k])

    eta_copies = [
        remote(eta.at[1], eta_rad.at[0], ETA_RAD, above),
        remote(eta.at[0], eta_rad.at[1], ETA_RAD + 1, below),
        remote(ceta, ceta_rad.at[0], COARSE_RAD, above),
        remote(ceta, ceta_rad.at[1], COARSE_RAD + 1, below),
        remote(eta_phi_send.at[0], eta_phi.at[0], ETA_PHI, right),
        remote(eta_phi_send.at[1], eta_phi.at[1], ETA_PHI + 1, left),
    ]
    first_copies = [
        remote(first, first_rad.at[0], FIRST_RAD, above),
        remote(first, first_rad.at[1], FIRST_RAD + 1, below),
        remote(first_phi_send.at[0], first_phi.at[0], FIRST_PHI, right),
        remote(first_phi_send.at[1], first_phi.at[1], FIRST_PHI + 1, left),
    ]

    def iota(shape, dim):
        return lax.broadcasted_iota(jnp.int32, shape, dim)

    lane, row = iota((width, na), 1), iota((width, na), 0)
    tile_lane = iota((width, half), 1)
    slot_lane = iota((8, WIN * CAP), 1)

    def shift(x, dim, up, fill):
        count = x.shape[dim]
        at = iota(x.shape, dim)
        rolled = pltpu.roll(x, count - 1 if up else 1, dim)
        return jnp.where(at == (count - 1 if up else 0), fill, rolled)

    def put_rim(k, packed):
        tall = jnp.concatenate([jnp.where(slot_lane // WIN == s, packed, 0.0) for s in range(CAP)], axis=0)
        turned = tall.T
        rows = turned[0:WIN]
        for s in range(1, CAP):
            rows = rows + turned[s * WIN : (s + 1) * WIN]
        rim_send[k, :, 0 : 8 * CAP] = rows

    def pack(field):
        found = exact_dot(field, onehot[...]).reshape(8, width, WIN * CAP)
        return jnp.sum(found * pick[...][None], axis=1)

    def put_edges(k):
        for c in range(4):
            for r in range(2):
                phi_send[k, 0, 2 * c + r, :] = cur[k, c, r, width - 1, :]
                phi_send[k, 1, 2 * c + r, :] = cur[k, c, r, 0, :]

    pairs = (iota((na, half), 0) // 2 == iota((na, half), 1)).astype(F32).astype(jnp.bfloat16)

    def fold_rows(count):
        return fold[pl.ds(0, count, stride=2), :] + fold[pl.ds(1, count, stride=2), :]

    rim_send[...] = jnp.zeros_like(rim_send)
    eta_phi_send[...] = jnp.zeros_like(eta_phi_send)
    loads[1].wait()
    loads[2].wait()
    mine = cel[pl.ds(lax.rem(lat + strips - WIN // 2 + 1, strips), WIN), :].astype(F32)
    lanes = iota((WIN, WIN * CAP), 1)
    spread = jnp.zeros((WIN, WIN * CAP), F32)
    for s in range(CAP):
        spread = jnp.where(lanes // WIN == s, mine[:, s : s + 1], spread)
    spread = jnp.where(lanes % WIN == iota((WIN, WIN * CAP), 0), spread, 0.0)
    cell = jnp.sum(spread, axis=0, keepdims=True).astype(jnp.int32)
    cell_lat, cell_lon = cell % na, cell // na
    onehot[...] = (iota((na, WIN * CAP), 0) == cell_lat).astype(F32).astype(jnp.bfloat16)
    in_lon = (iota((width, WIN * CAP), 0) == cell_lon).astype(F32)
    pick[...] = in_lon
    pick_edge[0] = jnp.where(cell_lat == 0, in_lon, 0.0)
    pick_edge[1] = jnp.where(cell_lat == na - 1, in_lon, 0.0)
    loads[0].wait()
    put_rim(0, pack(cur[0].reshape(8 * width, na)))
    put_edges(0)

    loads[3].wait()
    fold[0:width, :] = exact_dot(eta[0] + eta[1], pairs)
    coarse_eta = 0.125 * fold_rows(width // 2)
    ceta[...] = coarse_eta
    for r in range(2):
        eta_phi_send[0, r, :] = eta[r, width - 1, :]
        eta_phi_send[1, r, :] = eta[r, 0, :]
    eta_phi_send[0, 2, 0:half] = ceta[width // 2 - 1, :]
    eta_phi_send[1, 2, 0:half] = ceta[0, :]

    pl.semaphore_wait(barrier, WIN + 4)
    rim_start(0)
    for copy in rad_copies(0) + phi_copies(0) + eta_copies:
        copy.start()

    for load in loads[4:]:
        load.wait()
    lanes = iota((2 * width, WIN * CAP), 1)
    slot_here = lax.rem(lanes % WIN + lat + strips - WIN // 2, strips) * CAP + lanes // WIN
    total = jnp.zeros((2 * width, WIN * CAP), F32)
    for s in range(4):
        total = total + jnp.where(slt[:, s : s + 1] == slot_here, wgt[:, s : s + 1], 0.0)
    weigh[...] = total

    for copy in eta_copies:
        copy.wait_recv()
    eta_below = jnp.where(has_below, eta_rad[0], 0.0)
    eta_above = jnp.where(has_above, eta_rad[1], 0.0)
    w_rad[0] = 0.5 * (eta[0] + eta_below)
    w_rad[1] = 0.5 * (eta[0] + eta[1])
    w_rad[2] = 0.5 * (eta[1] + eta_above)
    for r in range(2):
        own = eta[r]
        low_row = jnp.where(has_left, eta_phi[0, r : r + 1, :], 0.0)
        high_row = jnp.where(has_right, eta_phi[1, r : r + 1, :], 0.0)
        phi_low = 0.5 * (own + shift(own, 0, False, low_row))
        phi_high = 0.5 * (own + shift(own, 0, True, high_row))
        lat_low = 0.5 * (own + shift(own, 1, False, own))
        lat_high = 0.5 * (own + shift(own, 1, True, own))
        inverse_eta = 1.0 / own
        w_phi[0, r], w_phi[1, r] = phi_low, phi_high
        w_lat[0, r], w_lat[1, r] = lat_low, lat_high
        inv_eta[r] = inverse_eta
        diag[r] = w_rad[r] + w_rad[r + 1] + (phi_low + phi_high) + (lat_low + lat_high)
        for e in range(2):
            at = 0 if e == 0 else na - 1

            def column(x, at=at):
                return jnp.broadcast_to(x[:, at : at + 1], (width, half))

            sign = 0.5 if e == 0 else -0.5
            w = column(lat_low if e == 0 else lat_high)
            ie = column(inverse_eta)
            edge_w[e, r], edge_ie[e, r] = w, ie
            for i in range(4):
                v = [OMEGA * column(vin[min(i, j), max(i, j), r]) for j in range(4)]
                gain[e, i, 0, r] = v[0] * w
                gain[e, i, 1, r] = v[1] * w
                gain[e, i, 2, r] = v[2] * w - sign * v[3]
                gain[e, i, 3, r] = v[3] * ie + sign * v[2]

    own = ceta[...]
    c_below = jnp.where(has_below, ceta_rad[0], 0.0)
    c_above = jnp.where(has_above, ceta_rad[1], 0.0)
    c_left = jnp.where(has_left, eta_phi[0, 2:3, 0:half], 0.0)
    c_right = jnp.where(has_right, eta_phi[1, 2:3, 0:half], 0.0)
    faces = [
        0.5 * (own + c_below), 0.5 * (own + c_above),
        0.5 * (own + shift(own, 0, False, c_left)), 0.5 * (own + shift(own, 0, True, c_right)),
        0.5 * (own + shift(own, 1, False, own)), 0.5 * (own + shift(own, 1, True, own)),
    ]
    for n, face in enumerate(faces):
        cfaces[n] = face
    faces_sum = (faces[0] + faces[1]) + (faces[2] + faces[3]) + (faces[4] + faces[5])
    cdia[0] = faces_sum
    cdia[1] = OMEGA / (0.25 * faces_sum)
    cdia[2] = OMEGA / (0.25 * (6.0 / own))
    cdia[3] = 1.0 / own

    def residual(k):
        result = [[None, None] for _ in range(4)]
        sums = [None, None]
        flows = [None, None]
        for r in range(2):
            v = [cur[k, c, r] for c in range(4)]
            other = [cur[k, c, 1 - r] for c in range(4)]
            lo = [shift(v[c], 1, False, 0.0) for c in range(4)]
            hi = [shift(v[c], 1, True, 0.0) for c in range(4)]
            for c in range(3):
                result[c][r] = (
                    frc[c, r] - diag[r] * v[c] + w_rad[1] * other[c] + w_lat[0, r] * lo[c] + w_lat[1, r] * hi[c]
                )
            result[2][r] = result[2][r] + 0.5 * (lo[3] - hi[3])
            sums[r] = other[3] + lo[3] + hi[3] - 6.0 * v[3]
            flows[r] = hi[2] - lo[2]
            if r == 0:
                result[0][r] = result[0][r] - 0.5 * other[3]
                flows[r] = flows[r] + other[0]
            else:
                result[0][r] = result[0][r] + 0.5 * other[3]
                flows[r] = flows[r] - other[0]
        for copy in phi_copies(k):
            copy.wait_recv()
        for r in range(2):
            lo, hi = [], []
            for c in range(4):
                v = cur[k, c, r]
                n = 2 * c + r
                lo.append(shift(v, 0, False, jnp.where(has_left, phi_recv[k, 0, n : n + 1, :], 0.0)))
                hi.append(shift(v, 0, True, jnp.where(has_right, phi_recv[k, 1, n : n + 1, :], 0.0)))
            for c in range(3):
                result[c][r] = result[c][r] + w_phi[0, r] * lo[c] + w_phi[1, r] * hi[c]
            result[1][r] = result[1][r] + 0.5 * (lo[3] - hi[3])
            sums[r] = sums[r] + lo[3] + hi[3]
            flows[r] = flows[r] + (hi[1] - lo[1])
        for copy in rad_copies(k):
            copy.wait_recv()
        for r in range(2):
            has, sign, w = (has_below, 0.5, w_rad[0]) if r == 0 else (has_above, -0.5, w_rad[2])
            n = [jnp.where(has, rad_recv[k, r, c], 0.0) for c in range(4)]
            for c in range(3):
                result[c][r] = result[c][r] + w * n[c]
            result[0][r] = result[0][r] + sign * n[3]
            flow = flows[r] - n[0] if r == 0 else flows[r] + n[0]
            result[3][r] = frc[3, r] + inv_eta[r] * (sums[r] + n[3]) + 0.5 * flow
        return result

    def ghosts(k):
        rim_all(k, recv_sem).wait()
        turned = rim_recv[k].T
        by_slot = jnp.concatenate([turned[8 * s : 8 * s + 8] for s in range(CAP)], axis=1)
        return jnp.sum(by_slot[:, None, :] * weigh[...][None], axis=-1, keepdims=True)

    def sent(k):
        for copy in rad_copies(k) + phi_copies(k):
            copy.wait_send()
        rim_all(k, send_sem).wait()

    def sweep(k, carry):
        res = residual(k)
        scaled = [[OMEGA * res[j][r] for r in range(2)] for j in range(4)]
        for i in range(4):
            for r in range(2):
                gained = cur[k, i, r]
                for j in range(4):
                    gained = gained + vin[min(i, j), max(i, j), r] * scaled[j][r]
                cur[k + 1, i, r] = gained
        packed = pack(cur[k + 1].reshape(8 * width, na))
        sent(k)
        ghost = ghosts(k)
        deltas = []
        for e in range(2):
            delta = []
            for i in range(4):
                for r in range(2):
                    value = jnp.zeros((width, half), F32)
                    for j in range(4):
                        value = value + gain[e, i, j, r] * ghost[2 * j + r, e * width : (e + 1) * width, :]
                    delta.append(value)
            deltas.append(delta)
        at_edge = jnp.stack(
            [deltas[0][n] * pick_edge[0] + deltas[1][n] * pick_edge[1] for n in range(8)], axis=0
        )
        put_rim(k + 1, packed + jnp.sum(at_edge, axis=1))
        rim_start(k + 1)
        for i in range(4):
            for r in range(2):
                n = 2 * i + r
                cur[k + 1, i, r, :, 0:half] += jnp.where(tile_lane == 0, deltas[0][n], 0.0)
                cur[k + 1, i, r, :, half:na] += jnp.where(tile_lane == half - 1, deltas[1][n], 0.0)
        put_edges(k + 1)
        for copy in rad_copies(k + 1) + phi_copies(k + 1):
            copy.start()
        return carry

    lax.fori_loop(0, SWEEPS, sweep, 0)
    store = pltpu.make_async_copy(cur.at[SWEEPS], iterate_out, local_sem.at[0])
    store.start()
    for copy in eta_copies:
        copy.wait_send()

    res = residual(SWEEPS)
    summed = jnp.concatenate([res[c][0] + res[c][1] for c in range(4)], axis=0)
    fold[...] = exact_dot(summed, pairs)
    base = fold_rows(4 * (width // 2))
    sent(SWEEPS)
    ghost = ghosts(SWEEPS)
    tops = []
    for e in range(2):
        sign = 0.5 if e == 0 else -0.5
        terms = [jnp.zeros((width, half), F32) for _ in range(4)]
        for r in range(2):
            g = [ghost[2 * j + r, e * width : (e + 1) * width, :] for j in range(4)]
            for c in range(3):
                terms[c] = terms[c] + edge_w[e, r] * g[c]
            terms[2] = terms[2] + sign * g[3]
            terms[3] = terms[3] + (edge_ie[e, r] * g[3] - sign * g[2])
        fold[...] = jnp.concatenate(terms, axis=0)
        tops.append(fold_rows(4 * (width // 2)))
    lanes = iota(base.shape, 1)
    coarse = base + jnp.where(lanes == 0, tops[0], 0.0) + jnp.where(lanes == half - 1, tops[1], 0.0)
    coarse = (0.125 * coarse).reshape(4, width // 2, half)
    for c in range(4):
        first[c] = coarse[c] * cdia[1 if c < 3 else 2]
    for c in range(4):
        first_phi_send[0, c, :] = first[c, width // 2 - 1, :]
        first_phi_send[1, c, :] = first[c, 0, :]
    for copy in first_copies:
        copy.start()
    one = [first[c] for c in range(4)]
    lat_lo = [shift(one[c], 1, False, 0.0) for c in range(4)]
    lat_hi = [shift(one[c], 1, True, 0.0) for c in range(4)]
    for copy in first_copies:
        copy.wait_recv()
    low, high = [], []
    low.append([jnp.where(has_below, first_rad[0, c], 0.0) for c in range(4)])
    high.append([jnp.where(has_above, first_rad[1, c], 0.0) for c in range(4)])
    low.append([shift(one[c], 0, False, jnp.where(has_left, first_phi[0, c : c + 1, :], 0.0)) for c in range(4)])
    high.append([shift(one[c], 0, True, jnp.where(has_right, first_phi[1, c : c + 1, :], 0.0)) for c in range(4)])
    low.append(lat_lo)
    high.append(lat_hi)
    pressure = 6.0 * one[3]
    flow = jnp.zeros_like(pressure)
    for d in range(3):
        pressure = pressure - low[d][3] - high[d][3]
        flow = flow + (high[d][d] - low[d][d])
    for c in range(3):
        friction = cdia[0] * one[c]
        for d in range(3):
            friction = friction - cfaces[2 * d] * low[d][c] - cfaces[2 * d + 1] * high[d][c]
        applied = 0.25 * friction + 0.25 * (high[c][3] - low[c][3])
        coarse_out[c] = one[c] + cdia[1] * (coarse[c] - applied)
    applied = 0.25 * pressure * cdia[3] - 0.25 * flow
    coarse_out[3] = one[3] + cdia[2] * (coarse[3] - applied)
    for copy in first_copies:
        copy.wait_send()
    store.wait()


def shards(strips, layers, iterate_in, forcing, viscosity, vanka_inverse, pack_cells, take_slot, take_weight):
    _, comps, radial, width, na = iterate_in.shape
    half = na // 2
    field = (comps, radial, width, na)
    slots = WIN * CAP
    rounds = SWEEPS + 1

    def vmem(*shape, dtype=F32):
        return pltpu.VMEM(shape, dtype)

    scratch = [
        vmem(rounds, *field), vmem(*field), vmem(radial, width, na), vmem(4, *field),
        vmem(2 * strips, CAP, dtype=jnp.int32), vmem(2 * width, 4, dtype=jnp.int32), vmem(2 * width, 4),
        vmem(na, slots, dtype=jnp.bfloat16), vmem(width, slots), vmem(2, width, slots), vmem(2 * width, slots),
        vmem(radial, width, na), vmem(2, radial, width, na), vmem(2, radial, width, na), vmem(3, width, na),
        vmem(radial, width, na), vmem(2, 4, 4, radial, width, half), vmem(2, radial, width, half),
        vmem(2, radial, width, half),
        vmem(rounds, WIN, 128), vmem(rounds, WIN, 128), vmem(rounds, 2, comps, width, na),
        vmem(rounds, 2, 2 * comps, na), vmem(rounds, 2, 2 * comps, na),
        vmem(2, width, na), vmem(2, 8, na), vmem(2, 8, na), vmem(width // 2, half), vmem(2, width // 2, half),
        vmem(4, width // 2, half), vmem(6, width // 2, half),
        vmem(comps, width // 2, half), vmem(2, comps, width // 2, half), vmem(2, comps, half), vmem(2, comps, half),
        vmem(comps * width, half),
        pltpu.SemaphoreType.DMA((11,)), pltpu.SemaphoreType.DMA((30,)), pltpu.SemaphoreType.DMA((30,)),
    ]
    anywhere = pl.BlockSpec(memory_space=pl.ANY)
    iterate, coarse = pl.pallas_call(
        functools.partial(kernel, strips, layers),
        out_shape=(
            jax.ShapeDtypeStruct(field, F32),
            jax.ShapeDtypeStruct((comps, width // 2, half), F32),
        ),
        in_specs=[anywhere] * 7,
        out_specs=(anywhere, pl.BlockSpec(memory_space=pltpu.VMEM)),
        scratch_shapes=scratch,
        compiler_params=pltpu.CompilerParams(
            collective_id=0, has_side_effects=True, vmem_limit_bytes=32 * 1024 * 1024
        ),
        cost_estimate=pl.CostEstimate(flops=8_000_000, bytes_accessed=1_000_000, transcendentals=0),
    )(
        iterate_in[0], forcing[0], viscosity[0], vanka_inverse[0], pack_cells[0, 0], take_slot[0, 0], take_weight[0, 0],
    )
    return iterate[None], coarse[None, :, None]


def solution(mesh):
    in_specs = (
        P("patch", None, "rad", "lat", None),
        P("patch", None, "rad", "lat", None),
        P("patch", "rad", "lat", None),
        P("patch", None, None, "rad", "lat", None),
        P("patch", "lat", None, None),
        P("patch", "lat", None, None),
        P("patch", "lat", None, None),
    )
    out_specs = (P("patch", None, "rad", "lat", None), P("patch", None, "rad", "lat", None))
    part = functools.partial(shards, mesh.shape["lat"], mesh.shape["rad"])
    return jax.shard_map(part, mesh=mesh, in_specs=in_specs, out_specs=out_specs, check_vma=False)
```

```python
import functools

import jax
import jax.numpy as jnp
from jax import lax
from jax.experimental import pallas as pl
from jax.experimental.pallas import tpu as pltpu
from jax.sharding import PartitionSpec as P

SWEEPS = 3
OMEGA = 0.8
WIN = 32
CAP = 4
RIM, RAD, PHI, ETA_RAD, COARSE_RAD, ETA_PHI, FIRST_RAD, FIRST_PHI = 0, 4, 12, 20, 22, 24, 26, 28
F32 = jnp.float32


def exact_dot(values, zero_one):
    high = values.astype(jnp.bfloat16)
    rest = values - high.astype(F32)
    middle = rest.astype(jnp.bfloat16)
    low = (rest - middle.astype(F32)).astype(jnp.bfloat16)
    dot = functools.partial(jnp.dot, preferred_element_type=F32)
    return dot(high, zero_one) + (dot(middle, zero_one) + dot(low, zero_one))


def kernel(
    strips, layers,
    iterate_hbm, forcing_hbm, eta_hbm, inverse_hbm, cells_hbm, slots_hbm, weights_hbm,
    iterate_out, coarse_out,
    cur, frc, eta, vin, cel, slt, wgt, takes,
    onehot, pick, pick_edge, weigh, diag, w_phi, w_lat, w_rad, inv_eta, gain, edge_w, edge_ie,
    rim_send, rim_recv, rad_recv, phi_send, phi_recv,
    eta_rad, eta_phi_send, eta_phi, ceta, ceta_rad, cdia, cfaces,
    first, first_rad, first_phi_send, first_phi, fold,
    local_sem, send_sem, recv_sem,
):
    patch, lat, rad = lax.axis_index("patch"), lax.axis_index("lat"), lax.axis_index("rad")
    _, _, width, na = frc.shape
    half = na // 2
    has_below, has_above = rad > 0, rad < layers - 1
    has_left, has_right = lat > 0, lat < strips - 1

    def neighbour(has, lat_step, rad_step):
        return (
            jnp.where(has, patch, 1 - patch),
            jnp.where(has, lat + lat_step, lat),
            jnp.where(has, rad + rad_step, rad),
        )

    below, above = neighbour(has_below, 0, -1), neighbour(has_above, 0, 1)
    left, right = neighbour(has_left, -1, 0), neighbour(has_right, 1, 0)
    at_above, at_right = jnp.where(has_above, 0, 1), jnp.where(has_right, 0, 1)
    at_below, at_left = jnp.where(has_below, 1, 0), jnp.where(has_left, 1, 0)

    def across(offset):
        return (1 - patch, lax.rem(lat + offset + strips, strips), rad)

    loads = [
        pltpu.make_async_copy(iterate_hbm, cur.at[0], local_sem.at[0]),
        pltpu.make_async_copy(cells_hbm, cel, local_sem.at[1]),
        pltpu.make_async_copy(eta_hbm, eta, local_sem.at[2]),
        pltpu.make_async_copy(slots_hbm, slt, local_sem.at[3]),
        pltpu.make_async_copy(weights_hbm, wgt, local_sem.at[4]),
        pltpu.make_async_copy(forcing_hbm, frc, local_sem.at[5]),
    ]
    for i in range(4):
        loads.append(
            pltpu.make_async_copy(
                inverse_hbm.at[i, pl.ds(i, 4 - i)], vin.at[i, pl.ds(i, 4 - i)], local_sem.at[6 + i]
            )
        )
    for load in loads:
        load.start()

    barrier = pltpu.get_barrier_semaphore()

    def greet(device):
        pl.semaphore_signal(barrier, inc=1, device_id=device, device_id_type=pl.DeviceIdType.MESH)

    for offset in sorted(range(-WIN // 2, WIN // 2), key=lambda o: -abs(o)):
        greet(across(offset))
    for device in (below, above, left, right):
        greet(device)

    def remote(src, dst, sem, device, landing=None):
        return pltpu.make_async_remote_copy(
            src_ref=src, dst_ref=dst, send_sem=send_sem.at[sem],
            recv_sem=recv_sem.at[sem if landing is None else landing],
            device_id=device, device_id_type=pl.DeviceIdType.MESH,
        )

    def pair(src_up, src_down, dst, sem, up, down, at_up, at_down):
        return [
            remote(src_up, dst.at[at_up], sem, up, sem + at_up),
            remote(src_down, dst.at[at_down], sem + 1, down, sem + at_down),
        ]

    def rad_pair(src_up, src_down, dst, sem):
        return pair(src_up, src_down, dst, sem, above, below, at_above, at_below)

    def phi_pair(src, dst, sem):
        return pair(src.at[0], src.at[1], dst, sem, right, left, at_right, at_left)

    def arrived(dst, sem):
        for side in range(2):
            pltpu.make_async_copy(dst.at[side], dst.at[side], recv_sem.at[sem + side]).wait()

    def rad_copies(k):
        return rad_pair(cur.at[k, :, 1], cur.at[k, :, 0], rad_recv.at[k], RAD + 2 * k)

    def phi_copies(k):
        return phi_pair(phi_send.at[k], phi_recv.at[k], PHI + 2 * k)

    def rim_start(k):
        for slot in sorted(range(WIN), key=lambda s: -abs(s - WIN // 2 + 1)):
            remote(
                rim_send.at[k, pl.ds(slot, 1)], rim_recv.at[k, pl.ds(WIN - 1 - slot, 1)], RIM + k,
                across(slot - WIN // 2 + 1),
            ).start()

    def rim_all(k, sem):
        return pltpu.make_async_copy(rim_recv.at[k], rim_recv.at[k], sem.at[RIM + k])

    eta_copies = (
        rad_pair(eta.at[1], eta.at[0], eta_rad, ETA_RAD)
        + rad_pair(ceta, ceta, ceta_rad, COARSE_RAD)
        + phi_pair(eta_phi_send, eta_phi, ETA_PHI)
    )
    first_copies = phi_pair(first_phi_send, first_phi, FIRST_PHI) + rad_pair(first, first, first_rad, FIRST_RAD)

    def iota(shape, dim):
        return lax.broadcasted_iota(jnp.int32, shape, dim)

    lane, row = iota((width, na), 1), iota((width, na), 0)
    tile_lane = iota((width, half), 1)
    slot_lane = iota((8, WIN * CAP), 1)

    def shift(x, dim, up, fill):
        count = x.shape[dim]
        at = iota(x.shape, dim)
        rolled = pltpu.roll(x, count - 1 if up else 1, dim)
        return jnp.where(at == (count - 1 if up else 0), fill, rolled)

    def put_rim(k, packed):
        tall = jnp.concatenate([jnp.where(slot_lane // WIN == s, packed, 0.0) for s in range(CAP)], axis=0)
        turned = tall.T
        rows = turned[0:WIN]
        for s in range(1, CAP):
            rows = rows + turned[s * WIN : (s + 1) * WIN]
        rim_send[k, :, 0 : 8 * CAP] = rows

    def pack(field):
        found = exact_dot(field, onehot[...]).reshape(8, width, WIN * CAP)
        return jnp.sum(found * pick[...][None], axis=1)

    def put_edges(k):
        for c in range(4):
            for r in range(2):
                phi_send[k, 0, 2 * c + r, :] = cur[k, c, r, width - 1, :]
                phi_send[k, 1, 2 * c + r, :] = cur[k, c, r, 0, :]

    pairs = (iota((na, half), 0) // 2 == iota((na, half), 1)).astype(F32).astype(jnp.bfloat16)

    def fold_rows(count):
        return fold[pl.ds(0, count, stride=2), :] + fold[pl.ds(1, count, stride=2), :]

    rim_send[...] = jnp.zeros_like(rim_send)
    eta_phi_send[...] = jnp.zeros_like(eta_phi_send)
    loads[1].wait()
    cells = cel[...].astype(F32)
    cells = jnp.concatenate([cells, cells], axis=1)
    spread = jnp.zeros((CAP, WIN * CAP), F32)
    begin = lat + strips - WIN // 2 + 1
    for s in range(CAP):
        here = (iota((CAP, WIN * CAP), 1) // WIN == s) & (iota((CAP, WIN * CAP), 0) == s)
        turn = lax.rem(WIN * s - begin + 4 * strips, 2 * strips)
        spread = jnp.where(here, pltpu.roll(cells, turn, 1), spread)
    cell = jnp.sum(spread, axis=0, keepdims=True).astype(jnp.int32)
    cell_lat, cell_lon = cell % na, cell // na
    onehot[...] = (iota((na, WIN * CAP), 0) == cell_lat).astype(F32).astype(jnp.bfloat16)
    in_lon = (iota((width, WIN * CAP), 0) == cell_lon).astype(F32)
    pick[...] = in_lon
    pick_edge[0] = jnp.where(cell_lat == 0, in_lon, 0.0)
    pick_edge[1] = jnp.where(cell_lat == na - 1, in_lon, 0.0)
    loads[0].wait()
    put_rim(0, pack(cur[0].reshape(8 * width, na)))
    put_edges(0)

    loads[2].wait()
    fold[0:width, :] = exact_dot(eta[0] + eta[1], pairs)
    coarse_eta = 0.125 * fold_rows(width // 2)
    ceta[...] = coarse_eta
    for r in range(2):
        eta_phi_send[0, r, :] = eta[r, width - 1, :]
        eta_phi_send[1, r, :] = eta[r, 0, :]
    eta_phi_send[0, 2, 0:half] = ceta[width // 2 - 1, :]
    eta_phi_send[1, 2, 0:half] = ceta[0, :]

    pl.semaphore_wait(barrier, WIN + 4)
    rim_start(0)
    for copy in rad_copies(0) + phi_copies(0) + eta_copies:
        copy.start()

    for load in loads[3:]:
        load.wait()
    takes[...] = jnp.zeros_like(takes)
    takes[0:4, 0 : 2 * width] = slt[...].astype(F32)
    takes[4:8, 0 : 2 * width] = wgt[...]
    columns = takes[...].T[0 : 2 * width]
    lanes = iota((2 * width, WIN * CAP), 1)
    slot_here = (lax.rem(lanes % WIN + lat + strips - WIN // 2, strips) * CAP + lanes // WIN).astype(F32)
    total = jnp.zeros((2 * width, WIN * CAP), F32)
    for s in range(4):
        total = total + jnp.where(columns[:, s : s + 1] == slot_here, columns[:, 4 + s : 5 + s], 0.0)
    weigh[...] = total

    arrived(eta_rad, ETA_RAD)
    arrived(ceta_rad, COARSE_RAD)
    arrived(eta_phi, ETA_PHI)
    eta_below = jnp.where(has_below, eta_rad[0], 0.0)
    eta_above = jnp.where(has_above, eta_rad[1], 0.0)
    w_rad[0] = 0.5 * (eta[0] + eta_below)
    w_rad[1] = 0.5 * (eta[0] + eta[1])
    w_rad[2] = 0.5 * (eta[1] + eta_above)
    for r in range(2):
        own = eta[r]
        low_row = jnp.where(has_left, eta_phi[0, r : r + 1, :], 0.0)
        high_row = jnp.where(has_right, eta_phi[1, r : r + 1, :], 0.0)
        phi_low = 0.5 * (own + shift(own, 0, False, low_row))
        phi_high = 0.5 * (own + shift(own, 0, True, high_row))
        lat_low = 0.5 * (own + shift(own, 1, False, own))
        lat_high = 0.5 * (own + shift(own, 1, True, own))
        inverse_eta = 1.0 / own
        w_phi[0, r], w_phi[1, r] = phi_low, phi_high
        w_lat[0, r], w_lat[1, r] = lat_low, lat_high
        inv_eta[r] = inverse_eta
        diag[r] = w_rad[r] + w_rad[r + 1] + (phi_low + phi_high) + (lat_low + lat_high)
        for e in range(2):
            at = 0 if e == 0 else na - 1

            def column(x, at=at):
                return jnp.broadcast_to(x[:, at : at + 1], (width, half))

            sign = 0.5 if e == 0 else -0.5
            w = column(lat_low if e == 0 else lat_high)
            ie = column(inverse_eta)
            edge_w[e, r], edge_ie[e, r] = w, ie
            for i in range(4):
                v = [OMEGA * column(vin[min(i, j), max(i, j), r]) for j in range(4)]
                gain[e, i, 0, r] = v[0] * w
                gain[e, i, 1, r] = v[1] * w
                gain[e, i, 2, r] = v[2] * w - sign * v[3]
                gain[e, i, 3, r] = v[3] * ie + sign * v[2]

    own = ceta[...]
    c_below = jnp.where(has_below, ceta_rad[0], 0.0)
    c_above = jnp.where(has_above, ceta_rad[1], 0.0)
    c_left = jnp.where(has_left, eta_phi[0, 2:3, 0:half], 0.0)
    c_right = jnp.where(has_right, eta_phi[1, 2:3, 0:half], 0.0)
    faces = [
        0.5 * (own + c_below), 0.5 * (own + c_above),
        0.5 * (own + shift(own, 0, False, c_left)), 0.5 * (own + shift(own, 0, True, c_right)),
        0.5 * (own + shift(own, 1, False, own)), 0.5 * (own + shift(own, 1, True, own)),
    ]
    for n, face in enumerate(faces):
        cfaces[n] = face
    faces_sum = (faces[0] + faces[1]) + (faces[2] + faces[3]) + (faces[4] + faces[5])
    cdia[0] = faces_sum
    cdia[1] = OMEGA / (0.25 * faces_sum)
    cdia[2] = OMEGA / (0.25 * (6.0 / own))
    cdia[3] = 1.0 / own

    def residual(k):
        result = [[None, None] for _ in range(4)]
        sums = [None, None]
        flows = [None, None]
        for r in range(2):
            v = [cur[k, c, r] for c in range(4)]
            other = [cur[k, c, 1 - r] for c in range(4)]
            lo = [shift(v[c], 1, False, 0.0) for c in range(4)]
            hi = [shift(v[c], 1, True, 0.0) for c in range(4)]
            for c in range(3):
                result[c][r] = (
                    frc[c, r] - diag[r] * v[c] + w_rad[1] * other[c] + w_lat[0, r] * lo[c] + w_lat[1, r] * hi[c]
                )
            result[2][r] = result[2][r] + 0.5 * (lo[3] - hi[3])
            sums[r] = other[3] + lo[3] + hi[3] - 6.0 * v[3]
            flows[r] = hi[2] - lo[2]
            if r == 0:
                result[0][r] = result[0][r] - 0.5 * other[3]
                flows[r] = flows[r] + other[0]
            else:
                result[0][r] = result[0][r] + 0.5 * other[3]
                flows[r] = flows[r] - other[0]
        arrived(phi_recv.at[k], PHI + 2 * k)
        for r in range(2):
            lo, hi = [], []
            for c in range(4):
                v = cur[k, c, r]
                n = 2 * c + r
                lo.append(shift(v, 0, False, jnp.where(has_left, phi_recv[k, 0, n : n + 1, :], 0.0)))
                hi.append(shift(v, 0, True, jnp.where(has_right, phi_recv[k, 1, n : n + 1, :], 0.0)))
            for c in range(3):
                result[c][r] = result[c][r] + w_phi[0, r] * lo[c] + w_phi[1, r] * hi[c]
            result[1][r] = result[1][r] + 0.5 * (lo[3] - hi[3])
            sums[r] = sums[r] + lo[3] + hi[3]
            flows[r] = flows[r] + (hi[1] - lo[1])
        arrived(rad_recv.at[k], RAD + 2 * k)
        for r in range(2):
            has, sign, w = (has_below, 0.5, w_rad[0]) if r == 0 else (has_above, -0.5, w_rad[2])
            n = [jnp.where(has, rad_recv[k, r, c], 0.0) for c in range(4)]
            for c in range(3):
                result[c][r] = result[c][r] + w * n[c]
            result[0][r] = result[0][r] + sign * n[3]
            flow = flows[r] - n[0] if r == 0 else flows[r] + n[0]
            result[3][r] = frc[3, r] + inv_eta[r] * (sums[r] + n[3]) + 0.5 * flow
        return result

    def ghosts(k):
        rim_all(k, recv_sem).wait()
        turned = rim_recv[k].T
        by_slot = jnp.concatenate([turned[8 * s : 8 * s + 8] for s in range(CAP)], axis=1)
        return jnp.sum(by_slot[:, None, :] * weigh[...][None], axis=-1, keepdims=True)

    def sent(k):
        for copy in rad_copies(k) + phi_copies(k):
            copy.wait_send()
        rim_all(k, send_sem).wait()

    def sweep(k, carry):
        res = residual(k)
        scaled = [[OMEGA * res[j][r] for r in range(2)] for j in range(4)]
        for i in range(4):
            for r in range(2):
                gained = cur[k, i, r]
                for j in range(4):
                    gained = gained + vin[min(i, j), max(i, j), r] * scaled[j][r]
                cur[k + 1, i, r] = gained
        packed = pack(cur[k + 1].reshape(8 * width, na))
        sent(k)
        ghost = ghosts(k)
        deltas = []
        for e in range(2):
            delta = []
            for i in range(4):
                for r in range(2):
                    value = jnp.zeros((width, half), F32)
                    for j in range(4):
                        value = value + gain[e, i, j, r] * ghost[2 * j + r, e * width : (e + 1) * width, :]
                    delta.append(value)
            deltas.append(delta)
        at_edge = jnp.stack(
            [deltas[0][n] * pick_edge[0] + deltas[1][n] * pick_edge[1] for n in range(8)], axis=0
        )
        put_rim(k + 1, packed + jnp.sum(at_edge, axis=1))
        rim_start(k + 1)
        for i in range(4):
            for r in range(2):
                n = 2 * i + r
                cur[k + 1, i, r, :, 0:half] += jnp.where(tile_lane == 0, deltas[0][n], 0.0)
                cur[k + 1, i, r, :, half:na] += jnp.where(tile_lane == half - 1, deltas[1][n], 0.0)
        put_edges(k + 1)
        for copy in rad_copies(k + 1) + phi_copies(k + 1):
            copy.start()
        return carry

    lax.fori_loop(0, SWEEPS, sweep, 0)
    store = pltpu.make_async_copy(cur.at[SWEEPS], iterate_out, local_sem.at[0])
    store.start()
    for copy in eta_copies:
        copy.wait_send()

    res = residual(SWEEPS)
    summed = jnp.concatenate([res[c][0] + res[c][1] for c in range(4)], axis=0)
    fold[...] = exact_dot(summed, pairs)
    base = fold_rows(4 * (width // 2))
    sent(SWEEPS)
    ghost = ghosts(SWEEPS)
    tops = []
    for e in range(2):
        sign = 0.5 if e == 0 else -0.5
        terms = [jnp.zeros((width, half), F32) for _ in range(4)]
        for r in range(2):
            g = [ghost[2 * j + r, e * width : (e + 1) * width, :] for j in range(4)]
            for c in range(3):
                terms[c] = terms[c] + edge_w[e, r] * g[c]
            terms[2] = terms[2] + sign * g[3]
            terms[3] = terms[3] + (edge_ie[e, r] * g[3] - sign * g[2])
        fold[...] = jnp.concatenate(terms, axis=0)
        tops.append(fold_rows(4 * (width // 2)))
    lanes = iota(base.shape, 1)
    coarse = base + jnp.where(lanes == 0, tops[0], 0.0) + jnp.where(lanes == half - 1, tops[1], 0.0)
    coarse = (0.125 * coarse).reshape(4, width // 2, half)
    for c in range(4):
        first[c] = coarse[c] * cdia[1 if c < 3 else 2]
    for c in range(4):
        first_phi_send[0, c, :] = first[c, width // 2 - 1, :]
        first_phi_send[1, c, :] = first[c, 0, :]
    for copy in first_copies:
        copy.start()
    one = [first[c] for c in range(4)]
    lat_lo = [shift(one[c], 1, False, 0.0) for c in range(4)]
    lat_hi = [shift(one[c], 1, True, 0.0) for c in range(4)]
    arrived(first_phi, FIRST_PHI)
    arrived(first_rad, FIRST_RAD)
    low, high = [], []
    low.append([jnp.where(has_below, first_rad[0, c], 0.0) for c in range(4)])
    high.append([jnp.where(has_above, first_rad[1, c], 0.0) for c in range(4)])
    low.append([shift(one[c], 0, False, jnp.where(has_left, first_phi[0, c : c + 1, :], 0.0)) for c in range(4)])
    high.append([shift(one[c], 0, True, jnp.where(has_right, first_phi[1, c : c + 1, :], 0.0)) for c in range(4)])
    low.append(lat_lo)
    high.append(lat_hi)
    pressure = 6.0 * one[3]
    flow = jnp.zeros_like(pressure)
    for d in range(3):
        pressure = pressure - low[d][3] - high[d][3]
        flow = flow + (high[d][d] - low[d][d])
    for c in range(3):
        friction = cdia[0] * one[c]
        for d in range(3):
            friction = friction - cfaces[2 * d] * low[d][c] - cfaces[2 * d + 1] * high[d][c]
        applied = 0.25 * friction + 0.25 * (high[c][3] - low[c][3])
        coarse_out[c] = one[c] + cdia[1] * (coarse[c] - applied)
    applied = 0.25 * pressure * cdia[3] - 0.25 * flow
    coarse_out[3] = one[3] + cdia[2] * (coarse[3] - applied)
    for copy in first_copies:
        copy.wait_send()
    store.wait()


def shards(strips, layers, iterate_in, forcing, viscosity, vanka_inverse, pack_cells, take_slot, take_weight):
    _, comps, radial, width, na = iterate_in.shape
    half = na // 2
    field = (comps, radial, width, na)
    slots = WIN * CAP
    rounds = SWEEPS + 1

    def vmem(*shape, dtype=F32):
        return pltpu.VMEM(shape, dtype)

    scratch = [
        vmem(rounds, *field), vmem(*field), vmem(radial, width, na), vmem(4, *field),
        vmem(CAP, strips, dtype=jnp.int32), vmem(4, 2 * width, dtype=jnp.int32), vmem(4, 2 * width), vmem(8, 128),
        vmem(na, slots, dtype=jnp.bfloat16), vmem(width, slots), vmem(2, width, slots), vmem(2 * width, slots),
        vmem(radial, width, na), vmem(2, radial, width, na), vmem(2, radial, width, na), vmem(3, width, na),
        vmem(radial, width, na), vmem(2, 4, 4, radial, width, half), vmem(2, radial, width, half),
        vmem(2, radial, width, half),
        vmem(rounds, WIN, 128), vmem(rounds, WIN, 128), vmem(rounds, 2, comps, width, na),
        vmem(rounds, 2, 2 * comps, na), vmem(rounds, 2, 2 * comps, na),
        vmem(2, width, na), vmem(2, 8, na), vmem(2, 8, na), vmem(width // 2, half), vmem(2, width // 2, half),
        vmem(4, width // 2, half), vmem(6, width // 2, half),
        vmem(comps, width // 2, half), vmem(2, comps, width // 2, half), vmem(2, comps, half), vmem(2, comps, half),
        vmem(comps * width, half),
        pltpu.SemaphoreType.DMA((11,)), pltpu.SemaphoreType.DMA((30,)), pltpu.SemaphoreType.DMA((30,)),
    ]
    anywhere = pl.BlockSpec(memory_space=pl.ANY)
    whole = pl.BlockSpec(memory_space=pltpu.HBM)
    iterate, coarse = pl.pallas_call(
        functools.partial(kernel, strips, layers),
        out_shape=(
            jax.ShapeDtypeStruct(field, F32),
            jax.ShapeDtypeStruct((comps, width // 2, half), F32),
        ),
        in_specs=[whole] * 7,
        out_specs=(anywhere, pl.BlockSpec(memory_space=pltpu.VMEM)),
        scratch_shapes=scratch,
        compiler_params=pltpu.CompilerParams(
            collective_id=0, has_side_effects=True, vmem_limit_bytes=60 * 1024 * 1024
        ),
        cost_estimate=pl.CostEstimate(flops=8_000_000, bytes_accessed=1_000_000, transcendentals=0),
    )(
        iterate_in[0], forcing[0], viscosity[0], vanka_inverse[0],
        pack_cells[0, 0].T, take_slot[0, 0].T, take_weight[0, 0].T,
    )
    return iterate[None], coarse[None, :, None]


def solution(mesh):
    in_specs = (
        P("patch", None, "rad", "lat", None),
        P("patch", None, "rad", "lat", None),
        P("patch", "rad", "lat", None),
        P("patch", None, None, "rad", "lat", None),
        P("patch", "lat", None, None),
        P("patch", "lat", None, None),
        P("patch", "lat", None, None),
    )
    out_specs = (P("patch", None, "rad", "lat", None), P("patch", None, "rad", "lat", None))
    part = functools.partial(shards, mesh.shape["lat"], mesh.shape["rad"])
    return jax.shard_map(part, mesh=mesh, in_specs=in_specs, out_specs=out_specs, check_vma=False)
```

```python
import functools

import jax
import jax.numpy as jnp
from jax import lax
from jax.experimental import pallas as pl
from jax.experimental.pallas import tpu as pltpu
from jax.sharding import PartitionSpec as P

SWEEPS = 3
OMEGA = 0.8
WIN = 32
CAP = 4
RIM, RAD, PHI, ETA_RAD, COARSE_RAD, ETA_PHI, FIRST_RAD, FIRST_PHI = 0, 4, 12, 20, 22, 24, 26, 28
F32 = jnp.float32


def exact_dot(values, zero_one):
    high = values.astype(jnp.bfloat16)
    rest = values - high.astype(F32)
    middle = rest.astype(jnp.bfloat16)
    low = (rest - middle.astype(F32)).astype(jnp.bfloat16)
    dot = functools.partial(jnp.dot, preferred_element_type=F32)
    return dot(high, zero_one) + (dot(middle, zero_one) + dot(low, zero_one))


def kernel(
    strips, layers,
    iterate_hbm, forcing_hbm, eta_hbm, inverse_hbm, cells_hbm, slots_hbm, weights_hbm,
    iterate_out, coarse_out,
    cur, frc, eta, vin, cel, slt, wgt, takes,
    onehot, pick, pick_edge, weigh, diag, w_phi, w_lat, w_rad, inv_eta, gain, edge_w, edge_ie,
    rim_send, rim_recv, rad_recv, phi_send, phi_recv,
    eta_rad, eta_phi_send, eta_phi, ceta, ceta_rad, cdia, cfaces,
    first, first_rad, first_phi_send, first_phi, fold,
    local_sem, send_sem, recv_sem,
):
    patch, lat, rad = lax.axis_index("patch"), lax.axis_index("lat"), lax.axis_index("rad")
    _, _, width, na = frc.shape
    half = na // 2
    has_below, has_above = rad > 0, rad < layers - 1
    has_left, has_right = lat > 0, lat < strips - 1

    def neighbour(has, lat_step, rad_step):
        return (
            jnp.where(has, patch, 1 - patch),
            jnp.where(has, lat + lat_step, lat),
            jnp.where(has, rad + rad_step, rad),
        )

    below, above = neighbour(has_below, 0, -1), neighbour(has_above, 0, 1)
    left, right = neighbour(has_left, -1, 0), neighbour(has_right, 1, 0)
    at_above, at_right = jnp.where(has_above, 0, 1), jnp.where(has_right, 0, 1)
    at_below, at_left = jnp.where(has_below, 1, 0), jnp.where(has_left, 1, 0)

    def across(offset):
        return (1 - patch, lax.rem(lat + offset + strips, strips), rad)

    loads = [
        pltpu.make_async_copy(iterate_hbm, cur.at[0], local_sem.at[0]),
        pltpu.make_async_copy(cells_hbm, cel, local_sem.at[1]),
        pltpu.make_async_copy(eta_hbm, eta, local_sem.at[2]),
        pltpu.make_async_copy(slots_hbm, slt, local_sem.at[3]),
        pltpu.make_async_copy(weights_hbm, wgt, local_sem.at[4]),
        pltpu.make_async_copy(forcing_hbm, frc, local_sem.at[5]),
    ]
    for i in range(4):
        loads.append(
            pltpu.make_async_copy(
                inverse_hbm.at[i, pl.ds(i, 4 - i)], vin.at[i, pl.ds(i, 4 - i)], local_sem.at[6 + i]
            )
        )
    for load in loads:
        load.start()

    barrier = pltpu.get_barrier_semaphore()

    def greet(device):
        pl.semaphore_signal(barrier, inc=1, device_id=device, device_id_type=pl.DeviceIdType.MESH)

    for offset in sorted(range(-WIN // 2, WIN // 2), key=lambda o: -abs(o)):
        greet(across(offset))
    for device in (below, above, left, right):
        greet(device)

    def remote(src, dst, sem, device, landing=None):
        return pltpu.make_async_remote_copy(
            src_ref=src, dst_ref=dst, send_sem=send_sem.at[sem],
            recv_sem=recv_sem.at[sem if landing is None else landing],
            device_id=device, device_id_type=pl.DeviceIdType.MESH,
        )

    def pair(src_up, src_down, dst, sem, up, down, at_up, at_down):
        return [
            remote(src_up, dst.at[at_up], sem, up, sem + at_up),
            remote(src_down, dst.at[at_down], sem + 1, down, sem + at_down),
        ]

    def rad_pair(src_up, src_down, dst, sem):
        return pair(src_up, src_down, dst, sem, above, below, at_above, at_below)

    def phi_pair(src, dst, sem):
        return pair(src.at[0], src.at[1], dst, sem, right, left, at_right, at_left)

    def arrived(dst, sem):
        for side in range(2):
            pltpu.make_async_copy(dst.at[side], dst.at[side], recv_sem.at[sem + side]).wait()

    def rad_copies(k):
        return rad_pair(cur.at[k, :, 1], cur.at[k, :, 0], rad_recv.at[k], RAD + 2 * k)

    def phi_copies(k):
        return phi_pair(phi_send.at[k], phi_recv.at[k], PHI + 2 * k)

    def rim_start(k):
        for slot in sorted(range(WIN), key=lambda s: -abs(s - WIN // 2 + 1)):
            remote(
                rim_send.at[k, pl.ds(slot, 1)], rim_recv.at[k, pl.ds(WIN - 1 - slot, 1)], RIM + k,
                across(slot - WIN // 2 + 1),
            ).start()

    def rim_all(k, sem):
        return pltpu.make_async_copy(rim_recv.at[k], rim_recv.at[k], sem.at[RIM + k])

    eta_copies = (
        rad_pair(eta.at[1], eta.at[0], eta_rad, ETA_RAD)
        + rad_pair(ceta, ceta, ceta_rad, COARSE_RAD)
        + phi_pair(eta_phi_send, eta_phi, ETA_PHI)
    )
    first_copies = phi_pair(first_phi_send, first_phi, FIRST_PHI) + rad_pair(first, first, first_rad, FIRST_RAD)

    def iota(shape, dim):
        return lax.broadcasted_iota(jnp.int32, shape, dim)

    lane, row = iota((width, na), 1), iota((width, na), 0)
    tile_lane = iota((width, half), 1)
    slot_lane = iota((8, WIN * CAP), 1)

    def shift(x, dim, up, fill):
        count = x.shape[dim]
        at = iota(x.shape, dim)
        rolled = pltpu.roll(x, count - 1 if up else 1, dim)
        return jnp.where(at == (count - 1 if up else 0), fill, rolled)

    def put_rim(k, packed):
        tall = jnp.concatenate([jnp.where(slot_lane // WIN == s, packed, 0.0) for s in range(CAP)], axis=0)
        turned = tall.T
        rows = turned[0:WIN]
        for s in range(1, CAP):
            rows = rows + turned[s * WIN : (s + 1) * WIN]
        rim_send[k, :, 0 : 8 * CAP] = rows

    def pack(field):
        found = exact_dot(field, onehot[...]).reshape(8, width, WIN * CAP)
        return jnp.sum(found * pick[...][None], axis=1)

    def put_edges(k):
        for c in range(4):
            for r in range(2):
                phi_send[k, 0, 2 * c + r, :] = cur[k, c, r, width - 1, :]
                phi_send[k, 1, 2 * c + r, :] = cur[k, c, r, 0, :]

    pairs = (iota((na, half), 0) // 2 == iota((na, half), 1)).astype(F32).astype(jnp.bfloat16)

    def fold_rows(count):
        return fold[pl.ds(0, count, stride=2), :] + fold[pl.ds(1, count, stride=2), :]

    rim_send[...] = jnp.zeros_like(rim_send)
    eta_phi_send[...] = jnp.zeros_like(eta_phi_send)
    loads[1].wait()
    cells = cel[...].astype(F32)
    cells = jnp.concatenate([cells, cells], axis=1)
    spread = jnp.zeros((CAP, WIN * CAP), F32)
    begin = lat + strips - WIN // 2 + 1
    for s in range(CAP):
        here = (iota((CAP, WIN * CAP), 1) // WIN == s) & (iota((CAP, WIN * CAP), 0) == s)
        turn = lax.rem(WIN * s - begin + 4 * strips, 2 * strips)
        spread = jnp.where(here, pltpu.roll(cells, turn, 1), spread)
    cell = jnp.sum(spread, axis=0, keepdims=True).astype(jnp.int32)
    cell_lat, cell_lon = cell % na, cell // na
    onehot[...] = (iota((na, WIN * CAP), 0) == cell_lat).astype(F32).astype(jnp.bfloat16)
    in_lon = (iota((width, WIN * CAP), 0) == cell_lon).astype(F32)
    pick[...] = in_lon
    pick_edge[0] = jnp.where(cell_lat == 0, in_lon, 0.0)
    pick_edge[1] = jnp.where(cell_lat == na - 1, in_lon, 0.0)
    loads[0].wait()
    put_rim(0, pack(cur[0].reshape(8 * width, na)))
    put_edges(0)

    loads[2].wait()
    fold[0:width, :] = exact_dot(eta[0] + eta[1], pairs)
    coarse_eta = 0.125 * fold_rows(width // 2)
    ceta[...] = coarse_eta
    for r in range(2):
        eta_phi_send[0, r, :] = eta[r, width - 1, :]
        eta_phi_send[1, r, :] = eta[r, 0, :]
    eta_phi_send[0, 2, 0:half] = ceta[width // 2 - 1, :]
    eta_phi_send[1, 2, 0:half] = ceta[0, :]

    pl.semaphore_wait(barrier, WIN + 4)
    rim_start(0)
    for copy in rad_copies(0) + phi_copies(0) + eta_copies:
        copy.start()

    for load in loads[3:]:
        load.wait()
    takes[...] = jnp.zeros_like(takes)
    takes[0:4, 0 : 2 * width] = slt[...].astype(F32)
    takes[4:8, 0 : 2 * width] = wgt[...]
    columns = takes[...].T[0 : 2 * width]
    lanes = iota((2 * width, WIN * CAP), 1)
    slot_here = (lax.rem(lanes % WIN + lat + strips - WIN // 2, strips) * CAP + lanes // WIN).astype(F32)
    total = jnp.zeros((2 * width, WIN * CAP), F32)
    for s in range(4):
        total = total + jnp.where(columns[:, s : s + 1] == slot_here, columns[:, 4 + s : 5 + s], 0.0)
    weigh[...] = total

    arrived(eta_rad, ETA_RAD)
    arrived(ceta_rad, COARSE_RAD)
    arrived(eta_phi, ETA_PHI)
    eta_below = jnp.where(has_below, eta_rad[0], 0.0)
    eta_above = jnp.where(has_above, eta_rad[1], 0.0)
    w_rad[0] = 0.5 * (eta[0] + eta_below)
    w_rad[1] = 0.5 * (eta[0] + eta[1])
    w_rad[2] = 0.5 * (eta[1] + eta_above)
    for r in range(2):
        own = eta[r]
        low_row = jnp.where(has_left, eta_phi[0, r : r + 1, :], 0.0)
        high_row = jnp.where(has_right, eta_phi[1, r : r + 1, :], 0.0)
        phi_low = 0.5 * (own + shift(own, 0, False, low_row))
        phi_high = 0.5 * (own + shift(own, 0, True, high_row))
        lat_low = 0.5 * (own + shift(own, 1, False, own))
        lat_high = 0.5 * (own + shift(own, 1, True, own))
        inverse_eta = 1.0 / own
        w_phi[0, r], w_phi[1, r] = phi_low, phi_high
        w_lat[0, r], w_lat[1, r] = lat_low, lat_high
        inv_eta[r] = inverse_eta
        diag[r] = w_rad[r] + w_rad[r + 1] + (phi_low + phi_high) + (lat_low + lat_high)
        for e in range(2):
            at = 0 if e == 0 else na - 1

            def column(x, at=at):
                return jnp.broadcast_to(x[:, at : at + 1], (width, half))

            sign = 0.5 if e == 0 else -0.5
            w = column(lat_low if e == 0 else lat_high)
            ie = column(inverse_eta)
            edge_w[e, r], edge_ie[e, r] = w, ie
            for i in range(4):
                v = [OMEGA * column(vin[min(i, j), max(i, j), r]) for j in range(4)]
                gain[e, i, 0, r] = v[0] * w
                gain[e, i, 1, r] = v[1] * w
                gain[e, i, 2, r] = v[2] * w - sign * v[3]
                gain[e, i, 3, r] = v[3] * ie + sign * v[2]

    own = ceta[...]
    c_below = jnp.where(has_below, ceta_rad[0], 0.0)
    c_above = jnp.where(has_above, ceta_rad[1], 0.0)
    c_left = jnp.where(has_left, eta_phi[0, 2:3, 0:half], 0.0)
    c_right = jnp.where(has_right, eta_phi[1, 2:3, 0:half], 0.0)
    faces = [
        0.5 * (own + c_below), 0.5 * (own + c_above),
        0.5 * (own + shift(own, 0, False, c_left)), 0.5 * (own + shift(own, 0, True, c_right)),
        0.5 * (own + shift(own, 1, False, own)), 0.5 * (own + shift(own, 1, True, own)),
    ]
    for n, face in enumerate(faces):
        cfaces[n] = face
    faces_sum = (faces[0] + faces[1]) + (faces[2] + faces[3]) + (faces[4] + faces[5])
    cdia[0] = faces_sum
    cdia[1] = OMEGA / (0.25 * faces_sum)
    cdia[2] = OMEGA / (0.25 * (6.0 / own))
    cdia[3] = 1.0 / own

    def residual(k):
        result = [[None, None] for _ in range(4)]
        sums = [None, None]
        flows = [None, None]
        for r in range(2):
            v = [cur[k, c, r] for c in range(4)]
            other = [cur[k, c, 1 - r] for c in range(4)]
            lo = [shift(v[c], 1, False, 0.0) for c in range(4)]
            hi = [shift(v[c], 1, True, 0.0) for c in range(4)]
            for c in range(3):
                result[c][r] = (
                    frc[c, r] - diag[r] * v[c] + w_rad[1] * other[c] + w_lat[0, r] * lo[c] + w_lat[1, r] * hi[c]
                )
            result[2][r] = result[2][r] + 0.5 * (lo[3] - hi[3])
            sums[r] = other[3] + lo[3] + hi[3] - 6.0 * v[3]
            flows[r] = hi[2] - lo[2]
            if r == 0:
                result[0][r] = result[0][r] - 0.5 * other[3]
                flows[r] = flows[r] + other[0]
            else:
                result[0][r] = result[0][r] + 0.5 * other[3]
                flows[r] = flows[r] - other[0]
        arrived(phi_recv.at[k], PHI + 2 * k)
        for r in range(2):
            lo, hi = [], []
            for c in range(4):
                v = cur[k, c, r]
                n = 2 * c + r
                lo.append(shift(v, 0, False, jnp.where(has_left, phi_recv[k, 0, n : n + 1, :], 0.0)))
                hi.append(shift(v, 0, True, jnp.where(has_right, phi_recv[k, 1, n : n + 1, :], 0.0)))
            for c in range(3):
                result[c][r] = result[c][r] + w_phi[0, r] * lo[c] + w_phi[1, r] * hi[c]
            result[1][r] = result[1][r] + 0.5 * (lo[3] - hi[3])
            sums[r] = sums[r] + lo[3] + hi[3]
            flows[r] = flows[r] + (hi[1] - lo[1])
        arrived(rad_recv.at[k], RAD + 2 * k)
        for r in range(2):
            has, sign, w = (has_below, 0.5, w_rad[0]) if r == 0 else (has_above, -0.5, w_rad[2])
            n = [jnp.where(has, rad_recv[k, r, c], 0.0) for c in range(4)]
            for c in range(3):
                result[c][r] = result[c][r] + w * n[c]
            result[0][r] = result[0][r] + sign * n[3]
            flow = flows[r] - n[0] if r == 0 else flows[r] + n[0]
            result[3][r] = frc[3, r] + inv_eta[r] * (sums[r] + n[3]) + 0.5 * flow
        return result

    def ghosts(k):
        rim_all(k, recv_sem).wait()
        turned = rim_recv[k].T
        by_slot = jnp.concatenate([turned[8 * s : 8 * s + 8] for s in range(CAP)], axis=1)
        return jnp.sum(by_slot[:, None, :] * weigh[...][None], axis=-1, keepdims=True)

    def sent(k):
        for copy in rad_copies(k) + phi_copies(k):
            copy.wait_send()
        rim_all(k, send_sem).wait()

    def sweep(k, carry):
        res = residual(k)
        scaled = [[OMEGA * res[j][r] for r in range(2)] for j in range(4)]
        for i in range(4):
            for r in range(2):
                gained = cur[k, i, r]
                for j in range(4):
                    gained = gained + vin[min(i, j), max(i, j), r] * scaled[j][r]
                cur[k + 1, i, r] = gained
        packed = pack(cur[k + 1].reshape(8 * width, na))
        sent(k)
        ghost = ghosts(k)
        deltas = []
        for e in range(2):
            delta = []
            for i in range(4):
                for r in range(2):
                    value = jnp.zeros((width, half), F32)
                    for j in range(4):
                        value = value + gain[e, i, j, r] * ghost[2 * j + r, e * width : (e + 1) * width, :]
                    delta.append(value)
            deltas.append(delta)
        at_edge = jnp.stack(
            [deltas[0][n] * pick_edge[0] + deltas[1][n] * pick_edge[1] for n in range(8)], axis=0
        )
        put_rim(k + 1, packed + jnp.sum(at_edge, axis=1))
        rim_start(k + 1)
        for i in range(4):
            for r in range(2):
                n = 2 * i + r
                cur[k + 1, i, r, :, 0:half] += jnp.where(tile_lane == 0, deltas[0][n], 0.0)
                cur[k + 1, i, r, :, half:na] += jnp.where(tile_lane == half - 1, deltas[1][n], 0.0)
        put_edges(k + 1)
        for copy in rad_copies(k + 1) + phi_copies(k + 1):
            copy.start()
        return carry

    lax.fori_loop(0, SWEEPS, sweep, 0)
    store = pltpu.make_async_copy(cur.at[SWEEPS], iterate_out, local_sem.at[0])
    store.start()
    for copy in eta_copies:
        copy.wait_send()

    res = residual(SWEEPS)
    summed = jnp.concatenate([res[c][0] + res[c][1] for c in range(4)], axis=0)
    fold[...] = exact_dot(summed, pairs)
    base = fold_rows(4 * (width // 2))
    sent(SWEEPS)
    ghost = ghosts(SWEEPS)
    tops = []
    for e in range(2):
        sign = 0.5 if e == 0 else -0.5
        terms = [jnp.zeros((width, half), F32) for _ in range(4)]
        for r in range(2):
            g = [ghost[2 * j + r, e * width : (e + 1) * width, :] for j in range(4)]
            for c in range(3):
                terms[c] = terms[c] + edge_w[e, r] * g[c]
            terms[2] = terms[2] + sign * g[3]
            terms[3] = terms[3] + (edge_ie[e, r] * g[3] - sign * g[2])
        fold[...] = jnp.concatenate(terms, axis=0)
        tops.append(fold_rows(4 * (width // 2)))
    lanes = iota(base.shape, 1)
    coarse = base + jnp.where(lanes == 0, tops[0], 0.0) + jnp.where(lanes == half - 1, tops[1], 0.0)
    coarse = (0.125 * coarse).reshape(4, width // 2, half)
    for c in range(4):
        first[c] = coarse[c] * cdia[1 if c < 3 else 2]
    for c in range(4):
        first_phi_send[0, c, :] = first[c, width // 2 - 1, :]
        first_phi_send[1, c, :] = first[c, 0, :]
    for copy in first_copies:
        copy.start()
    one = [first[c] for c in range(4)]
    lat_lo = [shift(one[c], 1, False, 0.0) for c in range(4)]
    lat_hi = [shift(one[c], 1, True, 0.0) for c in range(4)]
    arrived(first_phi, FIRST_PHI)
    arrived(first_rad, FIRST_RAD)
    low, high = [], []
    low.append([jnp.where(has_below, first_rad[0, c], 0.0) for c in range(4)])
    high.append([jnp.where(has_above, first_rad[1, c], 0.0) for c in range(4)])
    low.append([shift(one[c], 0, False, jnp.where(has_left, first_phi[0, c : c + 1, :], 0.0)) for c in range(4)])
    high.append([shift(one[c], 0, True, jnp.where(has_right, first_phi[1, c : c + 1, :], 0.0)) for c in range(4)])
    low.append(lat_lo)
    high.append(lat_hi)
    pressure = 6.0 * one[3]
    flow = jnp.zeros_like(pressure)
    for d in range(3):
        pressure = pressure - low[d][3] - high[d][3]
        flow = flow + (high[d][d] - low[d][d])
    for c in range(3):
        friction = cdia[0] * one[c]
        for d in range(3):
            friction = friction - cfaces[2 * d] * low[d][c] - cfaces[2 * d + 1] * high[d][c]
        applied = 0.25 * friction + 0.25 * (high[c][3] - low[c][3])
        coarse_out[c] = one[c] + cdia[1] * (coarse[c] - applied)
    applied = 0.25 * pressure * cdia[3] - 0.25 * flow
    coarse_out[3] = one[3] + cdia[2] * (coarse[3] - applied)
    for copy in first_copies:
        copy.wait_send()
    store.wait()


def write_out(iterate, coarse, iterate_out, coarse_out, sem):
    copies = [
        pltpu.make_async_copy(iterate, iterate_out, sem.at[0]),
        pltpu.make_async_copy(coarse, coarse_out, sem.at[1]),
    ]
    for copy in copies:
        copy.start()
    for copy in copies:
        copy.wait()


def shards(strips, layers, iterate_in, forcing, viscosity, vanka_inverse, pack_cells, take_slot, take_weight):
    _, comps, radial, width, na = iterate_in.shape
    half = na // 2
    field = (comps, radial, width, na)
    slots = WIN * CAP
    rounds = SWEEPS + 1

    def vmem(*shape, dtype=F32):
        return pltpu.VMEM(shape, dtype)

    scratch = [
        vmem(rounds, *field), vmem(*field), vmem(radial, width, na), vmem(4, *field),
        vmem(CAP, strips, dtype=jnp.int32), vmem(4, 2 * width, dtype=jnp.int32), vmem(4, 2 * width), vmem(8, 128),
        vmem(na, slots, dtype=jnp.bfloat16), vmem(width, slots), vmem(2, width, slots), vmem(2 * width, slots),
        vmem(radial, width, na), vmem(2, radial, width, na), vmem(2, radial, width, na), vmem(3, width, na),
        vmem(radial, width, na), vmem(2, 4, 4, radial, width, half), vmem(2, radial, width, half),
        vmem(2, radial, width, half),
        vmem(rounds, WIN, 128), vmem(rounds, WIN, 128), vmem(rounds, 2, comps, width, na),
        vmem(rounds, 2, 2 * comps, na), vmem(rounds, 2, 2 * comps, na),
        vmem(2, width, na), vmem(2, 8, na), vmem(2, 8, na), vmem(width // 2, half), vmem(2, width // 2, half),
        vmem(4, width // 2, half), vmem(6, width // 2, half),
        vmem(comps, width // 2, half), vmem(2, comps, width // 2, half), vmem(2, comps, half), vmem(2, comps, half),
        vmem(comps * width, half),
        pltpu.SemaphoreType.DMA((11,)), pltpu.SemaphoreType.DMA((30,)), pltpu.SemaphoreType.DMA((30,)),
    ]
    anywhere = pl.BlockSpec(memory_space=pl.ANY)
    whole = pl.BlockSpec(memory_space=pltpu.HBM)
    iterate, coarse = pl.pallas_call(
        functools.partial(kernel, strips, layers),
        out_shape=(
            pltpu.VMEM(field, F32),
            pltpu.VMEM((comps, width // 2, half), F32),
        ),
        in_specs=[whole] * 7,
        out_specs=(pl.BlockSpec(memory_space=pltpu.VMEM),) * 2,
        scratch_shapes=scratch,
        compiler_params=pltpu.CompilerParams(
            collective_id=0, has_side_effects=True, vmem_limit_bytes=60 * 1024 * 1024
        ),
        cost_estimate=pl.CostEstimate(flops=8_000_000, bytes_accessed=1_000_000, transcendentals=0),
    )(
        iterate_in[0], forcing[0], viscosity[0], vanka_inverse[0],
        pack_cells[0, 0].T, take_slot[0, 0].T, take_weight[0, 0].T,
    )
    iterate, coarse = pl.pallas_call(
        write_out,
        out_shape=(
            jax.ShapeDtypeStruct(field, F32),
            jax.ShapeDtypeStruct((comps, width // 2, half), F32),
        ),
        in_specs=[pl.BlockSpec(memory_space=pltpu.VMEM)] * 2,
        out_specs=(whole, whole),
        scratch_shapes=[pltpu.SemaphoreType.DMA((2,))],
    )(*(pltpu.with_memory_space_constraint(x, pltpu.VMEM) for x in (iterate, coarse)))
    return iterate[None], coarse[None, :, None]


def solution(mesh):
    in_specs = (
        P("patch", None, "rad", "lat", None),
        P("patch", None, "rad", "lat", None),
        P("patch", "rad", "lat", None),
        P("patch", None, None, "rad", "lat", None),
        P("patch", "lat", None, None),
        P("patch", "lat", None, None),
        P("patch", "lat", None, None),
    )
    out_specs = (P("patch", None, "rad", "lat", None), P("patch", None, "rad", "lat", None))
    part = functools.partial(shards, mesh.shape["lat"], mesh.shape["rad"])
    return jax.shard_map(part, mesh=mesh, in_specs=in_specs, out_specs=out_specs, check_vma=False)
```

```python
import functools

import jax
import jax.numpy as jnp
from jax import lax
from jax.experimental import pallas as pl
from jax.experimental.pallas import tpu as pltpu
from jax.sharding import PartitionSpec as P

SWEEPS = 3
OMEGA = 0.8
WIN = 32
CAP = 4
RIM, RAD, PHI, ETA_RAD, COARSE_RAD, ETA_PHI, FIRST_RAD, FIRST_PHI = 0, 4, 12, 20, 22, 24, 26, 28
F32 = jnp.float32


def exact_dot(values, zero_one):
    high = values.astype(jnp.bfloat16)
    rest = values - high.astype(F32)
    middle = rest.astype(jnp.bfloat16)
    low = (rest - middle.astype(F32)).astype(jnp.bfloat16)
    dot = functools.partial(jnp.dot, preferred_element_type=F32)
    return dot(high, zero_one) + (dot(middle, zero_one) + dot(low, zero_one))


def kernel(
    strips, layers,
    iterate_hbm, forcing_hbm, eta_hbm, inverse_hbm, cells_hbm, slots_hbm, weights_hbm,
    iterate_out, coarse_out,
    cur, frc, eta, vin, cel, slt, wgt,
    onehot, pick, pick_edge, take_at, take_by, slot_gain, diag, w_phi, w_lat, w_rad, inv_eta, gain, edge_w, edge_ie,
    rim_send, rim_recv, rad_recv, phi_send, phi_recv,
    eta_rad, eta_phi_send, eta_phi, ceta, ceta_rad, cdia, cfaces,
    first, first_rad, first_phi_send, first_phi, fold,
    local_sem, send_sem, recv_sem,
):
    patch, lat, rad = lax.axis_index("patch"), lax.axis_index("lat"), lax.axis_index("rad")
    _, _, width, na = frc.shape
    half = na // 2
    has_below, has_above = rad > 0, rad < layers - 1
    has_left, has_right = lat > 0, lat < strips - 1

    def neighbour(has, lat_step, rad_step):
        return (
            jnp.where(has, patch, 1 - patch),
            jnp.where(has, lat + lat_step, lat),
            jnp.where(has, rad + rad_step, rad),
        )

    below, above = neighbour(has_below, 0, -1), neighbour(has_above, 0, 1)
    left, right = neighbour(has_left, -1, 0), neighbour(has_right, 1, 0)
    at_above, at_right = jnp.where(has_above, 0, 1), jnp.where(has_right, 0, 1)
    at_below, at_left = jnp.where(has_below, 1, 0), jnp.where(has_left, 1, 0)

    def across(offset):
        return (1 - patch, lax.rem(lat + offset + strips, strips), rad)

    loads = [
        pltpu.make_async_copy(iterate_hbm, cur.at[0], local_sem.at[0]),
        pltpu.make_async_copy(cells_hbm, cel, local_sem.at[1]),
        pltpu.make_async_copy(eta_hbm, eta, local_sem.at[2]),
        pltpu.make_async_copy(slots_hbm, slt, local_sem.at[3]),
        pltpu.make_async_copy(weights_hbm, wgt, local_sem.at[4]),
        pltpu.make_async_copy(forcing_hbm, frc, local_sem.at[5]),
    ]
    for i in range(4):
        loads.append(
            pltpu.make_async_copy(
                inverse_hbm.at[i, pl.ds(i, 4 - i)], vin.at[i, pl.ds(i, 4 - i)], local_sem.at[6 + i]
            )
        )
    for load in loads:
        load.start()

    barrier = pltpu.get_barrier_semaphore()

    def greet(device):
        pl.semaphore_signal(barrier, inc=1, device_id=device, device_id_type=pl.DeviceIdType.MESH)

    for offset in sorted(range(-WIN // 2, WIN // 2), key=lambda o: -abs(o)):
        greet(across(offset))
    for device in (below, above, left, right):
        greet(device)

    def remote(src, dst, sem, device, landing=None):
        return pltpu.make_async_remote_copy(
            src_ref=src, dst_ref=dst, send_sem=send_sem.at[sem],
            recv_sem=recv_sem.at[sem if landing is None else landing],
            device_id=device, device_id_type=pl.DeviceIdType.MESH,
        )

    def pair(src_up, src_down, dst, sem, up, down, at_up, at_down):
        return [
            remote(src_up, dst.at[at_up], sem, up, sem + at_up),
            remote(src_down, dst.at[at_down], sem + 1, down, sem + at_down),
        ]

    def rad_pair(src_up, src_down, dst, sem):
        return pair(src_up, src_down, dst, sem, above, below, at_above, at_below)

    def phi_pair(src, dst, sem):
        return pair(src.at[0], src.at[1], dst, sem, right, left, at_right, at_left)

    def arrived(dst, sem):
        for side in range(2):
            pltpu.make_async_copy(dst.at[side], dst.at[side], recv_sem.at[sem + side]).wait()

    def rad_copies(k):
        return rad_pair(cur.at[k, :, 1], cur.at[k, :, 0], rad_recv.at[k], RAD + 2 * k)

    def phi_copies(k):
        return phi_pair(phi_send.at[k], phi_recv.at[k], PHI + 2 * k)

    def rim_start(k):
        for slot in sorted(range(WIN), key=lambda s: -abs(s - WIN // 2 + 1)):
            remote(
                rim_send.at[k, pl.ds(slot, 1)], rim_recv.at[k, pl.ds(WIN - 1 - slot, 1)], RIM + k,
                across(slot - WIN // 2 + 1),
            ).start()

    def rim_all(k, sem):
        return pltpu.make_async_copy(rim_recv.at[k], rim_recv.at[k], sem.at[RIM + k])

    eta_copies = (
        rad_pair(eta.at[1], eta.at[0], eta_rad, ETA_RAD)
        + rad_pair(ceta, ceta, ceta_rad, COARSE_RAD)
        + phi_pair(eta_phi_send, eta_phi, ETA_PHI)
    )
    first_copies = phi_pair(first_phi_send, first_phi, FIRST_PHI) + rad_pair(first, first, first_rad, FIRST_RAD)

    def iota(shape, dim):
        return lax.broadcasted_iota(jnp.int32, shape, dim)

    lane, row = iota((width, na), 1), iota((width, na), 0)
    tile_lane = iota((width, half), 1)
    slot_lane = iota((8, WIN * CAP), 1)

    def shift(x, dim, up, fill):
        count = x.shape[dim]
        at = iota(x.shape, dim)
        rolled = pltpu.roll(x, count - 1 if up else 1, dim)
        return jnp.where(at == (count - 1 if up else 0), fill, rolled)

    def put_rim(k, packed):
        tall = jnp.concatenate([jnp.where(slot_lane // WIN == s, packed, 0.0) for s in range(CAP)], axis=0)
        turned = tall.T
        rows = turned[0:WIN]
        for s in range(1, CAP):
            rows = rows + turned[s * WIN : (s + 1) * WIN]
        rim_send[k, :, 0 : 8 * CAP] = rows

    def pack(field):
        found = exact_dot(field, onehot[...]).reshape(8, width, WIN * CAP)
        return jnp.sum(found * pick[...][None], axis=1)

    def put_edges(k):
        for c in range(4):
            for r in range(2):
                phi_send[k, 0, 2 * c + r, :] = cur[k, c, r, width - 1, :]
                phi_send[k, 1, 2 * c + r, :] = cur[k, c, r, 0, :]

    def take(x, index):
        return jnp.take_along_axis(x, index, axis=1, mode="promise_in_bounds")

    pairs = (iota((na, half), 0) // 2 == iota((na, half), 1)).astype(F32).astype(jnp.bfloat16)

    def fold_rows(n, count):
        return fold[n, pl.ds(0, count, stride=2), :] + fold[n, pl.ds(1, count, stride=2), :]

    rim_send[...] = jnp.zeros_like(rim_send)
    eta_phi_send[...] = jnp.zeros_like(eta_phi_send)
    loads[1].wait()
    cells = cel[...].astype(F32)
    cells = jnp.concatenate([cells, cells], axis=1)
    spread = jnp.zeros((CAP, WIN * CAP), F32)
    begin = lat + strips - WIN // 2 + 1
    for s in range(CAP):
        here = (iota((CAP, WIN * CAP), 1) // WIN == s) & (iota((CAP, WIN * CAP), 0) == s)
        turn = lax.rem(WIN * s - begin + 4 * strips, 2 * strips)
        spread = jnp.where(here, pltpu.roll(cells, turn, 1), spread)
    cell = jnp.sum(spread, axis=0, keepdims=True).astype(jnp.int32)
    cell_lat, cell_lon = cell % na, cell // na
    onehot[...] = (iota((na, WIN * CAP), 0) == cell_lat).astype(F32).astype(jnp.bfloat16)
    in_lon = (iota((width, WIN * CAP), 0) == cell_lon).astype(F32)
    pick[...] = in_lon
    pick_edge[0] = jnp.where(cell_lat == 0, in_lon, 0.0)
    pick_edge[1] = jnp.where(cell_lat == na - 1, in_lon, 0.0)
    loads[0].wait()
    put_rim(0, pack(cur[0].reshape(8 * width, na)))
    put_edges(0)

    loads[2].wait()
    fold[0, 0:width, :] = exact_dot(eta[0] + eta[1], pairs)
    coarse_eta = 0.125 * fold_rows(0, width // 2)
    ceta[...] = coarse_eta
    for r in range(2):
        eta_phi_send[0, r, :] = eta[r, width - 1, :]
        eta_phi_send[1, r, :] = eta[r, 0, :]
    eta_phi_send[0, 2, 0:half] = ceta[width // 2 - 1, :]
    eta_phi_send[1, 2, 0:half] = ceta[0, :]

    for load in loads[3:]:
        load.wait()
    slot = slt[...]
    strip = lax.rem(slot // CAP - lat + WIN // 2 + 2 * strips, strips)
    at = ((slot % CAP) * WIN + strip).astype(F32)
    idle = jnp.zeros((4, WIN * CAP - 2 * width), F32)
    at, by = jnp.concatenate([at, idle], axis=1), jnp.concatenate([wgt[...], idle], axis=1)
    table = jnp.concatenate([at, by], axis=0)
    beside_low, beside_high = cell_lat == 0, cell_lat == na - 1
    beside_at = jnp.where(beside_low, cell_lon, jnp.where(beside_high, cell_lon + width, 0))
    moved = take(table, jnp.broadcast_to(beside_at, (8, WIN * CAP)))
    for which, rows in ((0, table), (1, moved)):
        for n in range(4):
            take_at[which, n] = jnp.broadcast_to(rows[n : n + 1], (8, WIN * CAP)).astype(jnp.int32)
            weight = rows[4 + n : 5 + n]
            if which == 1:
                weight = jnp.where(beside_low | beside_high, weight, 0.0)
            take_by[which, n] = jnp.broadcast_to(weight, (8, WIN * CAP))

    for r in range(2):
        own = eta[r]
        lat_low = 0.5 * (own + shift(own, 1, False, own))
        lat_high = 0.5 * (own + shift(own, 1, True, own))
        inverse_eta = 1.0 / own
        w_lat[0, r], w_lat[1, r] = lat_low, lat_high
        inv_eta[r] = inverse_eta
        for e in range(2):
            at = 0 if e == 0 else na - 1

            def column(x, at=at):
                return jnp.broadcast_to(x[:, at : at + 1], (width, half))

            sign = 0.5 if e == 0 else -0.5
            w = column(lat_low if e == 0 else lat_high)
            ie = column(inverse_eta)
            edge_w[e, r], edge_ie[e, r] = w, ie
            for i in range(4):
                v = [OMEGA * column(vin[min(i, j), max(i, j), r]) for j in range(4)]
                gain[e, i, 0, r] = v[0] * w
                gain[e, i, 1, r] = v[1] * w
                gain[e, i, 2, r] = v[2] * w - sign * v[3]
                gain[e, i, 3, r] = v[3] * ie + sign * v[2]
    w_rad[1] = 0.5 * (eta[0] + eta[1])
    for d in range(4):
        rows = []
        for i in range(4):
            for r in range(2):
                j = (i + d) % 4
                rows.append(gain[0, i, j, r] * pick_edge[0] + gain[1, i, j, r] * pick_edge[1])
        slot_gain[d] = jnp.sum(jnp.stack(rows, axis=0), axis=1)

    pl.semaphore_wait(barrier, WIN + 4)
    rim_start(0)
    for copy in eta_copies + phi_copies(0) + rad_copies(0):
        copy.start()

    arrived(eta_rad, ETA_RAD)
    arrived(ceta_rad, COARSE_RAD)
    arrived(eta_phi, ETA_PHI)
    eta_below = jnp.where(has_below, eta_rad[0], 0.0)
    eta_above = jnp.where(has_above, eta_rad[1], 0.0)
    w_rad[0] = 0.5 * (eta[0] + eta_below)
    w_rad[2] = 0.5 * (eta[1] + eta_above)
    for r in range(2):
        own = eta[r]
        low_row = jnp.where(has_left, eta_phi[0, r : r + 1, :], 0.0)
        high_row = jnp.where(has_right, eta_phi[1, r : r + 1, :], 0.0)
        phi_low = 0.5 * (own + shift(own, 0, False, low_row))
        phi_high = 0.5 * (own + shift(own, 0, True, high_row))
        w_phi[0, r], w_phi[1, r] = phi_low, phi_high
        diag[r] = w_rad[r] + w_rad[r + 1] + (phi_low + phi_high) + (w_lat[0, r] + w_lat[1, r])

    def residual(k):
        result = [[None, None] for _ in range(4)]
        sums = [None, None]
        flows = [None, None]
        for r in range(2):
            v = [cur[k, c, r] for c in range(4)]
            other = [cur[k, c, 1 - r] for c in range(4)]
            lo = [shift(v[c], 1, False, 0.0) for c in range(4)]
            hi = [shift(v[c], 1, True, 0.0) for c in range(4)]
            for c in range(3):
                result[c][r] = (
                    frc[c, r] - diag[r] * v[c] + w_rad[1] * other[c] + w_lat[0, r] * lo[c] + w_lat[1, r] * hi[c]
                )
            result[2][r] = result[2][r] + 0.5 * (lo[3] - hi[3])
            sums[r] = other[3] + lo[3] + hi[3] - 6.0 * v[3]
            flows[r] = hi[2] - lo[2]
            if r == 0:
                result[0][r] = result[0][r] - 0.5 * other[3]
                flows[r] = flows[r] + other[0]
            else:
                result[0][r] = result[0][r] + 0.5 * other[3]
                flows[r] = flows[r] - other[0]
        arrived(phi_recv.at[k], PHI + 2 * k)
        for r in range(2):
            lo, hi = [], []
            for c in range(4):
                v = cur[k, c, r]
                n = 2 * c + r
                lo.append(shift(v, 0, False, jnp.where(has_left, phi_recv[k, 0, n : n + 1, :], 0.0)))
                hi.append(shift(v, 0, True, jnp.where(has_right, phi_recv[k, 1, n : n + 1, :], 0.0)))
            for c in range(3):
                result[c][r] = result[c][r] + w_phi[0, r] * lo[c] + w_phi[1, r] * hi[c]
            result[1][r] = result[1][r] + 0.5 * (lo[3] - hi[3])
            sums[r] = sums[r] + lo[3] + hi[3]
            flows[r] = flows[r] + (hi[1] - lo[1])
        arrived(rad_recv.at[k], RAD + 2 * k)
        for r in range(2):
            has, sign, w = (has_below, 0.5, w_rad[0]) if r == 0 else (has_above, -0.5, w_rad[2])
            n = [jnp.where(has, rad_recv[k, r, c], 0.0) for c in range(4)]
            for c in range(3):
                result[c][r] = result[c][r] + w * n[c]
            result[0][r] = result[0][r] + sign * n[3]
            flow = flows[r] - n[0] if r == 0 else flows[r] + n[0]
            result[3][r] = frc[3, r] + inv_eta[r] * (sums[r] + n[3]) + 0.5 * flow
        return result

    def received(k):
        rim_all(k, recv_sem).wait()
        turned = jnp.concatenate([rim_recv[k]] * CAP, axis=0).T
        by_slot = turned[0:8]
        for s in range(1, CAP):
            by_slot = jnp.where(slot_lane // WIN == s, turned[8 * s : 8 * s + 8], by_slot)
        return by_slot

    def interpolate(by_slot, which):
        terms = [take_by[which, n] * take(by_slot, take_at[which, n]) for n in range(4)]
        return (terms[0] + terms[1]) + (terms[2] + terms[3])

    def columns_of(ghost):
        down = iota((8, WIN * CAP), 0)
        result = []
        for n in range(8):
            line = jnp.broadcast_to(ghost[n : n + 1], (8, WIN * CAP))
            parts = [take(line, down + 8 * m) for m in range(2 * width // 8)]
            result.append([jnp.concatenate(parts[:2], axis=0), jnp.concatenate(parts[2:], axis=0)])
        return result

    def sent(k):
        for copy in rad_copies(k) + phi_copies(k):
            copy.wait_send()
        rim_all(k, send_sem).wait()

    def sweep(k, carry):
        res = residual(k)
        scaled = [[OMEGA * res[j][r] for r in range(2)] for j in range(4)]
        for i in range(4):
            for r in range(2):
                gained = cur[k, i, r]
                for j in range(4):
                    gained = gained + vin[min(i, j), max(i, j), r] * scaled[j][r]
                cur[k + 1, i, r] = gained
        packed = pack(cur[k + 1].reshape(8 * width, na))
        sent(k)
        by_slot = received(k)
        beside = interpolate(by_slot, 1)
        for d in range(4):
            turned = beside if d == 0 else pltpu.roll(beside, 8 - 2 * d, 0)
            packed = packed + slot_gain[d] * turned
        put_rim(k + 1, packed)
        rim_start(k + 1)
        ghost = columns_of(interpolate(by_slot, 0))
        deltas = []
        for e in range(2):
            delta = []
            for i in range(4):
                for r in range(2):
                    value = gain[e, i, 0, r] * ghost[r][e]
                    for j in range(1, 4):
                        value = value + gain[e, i, j, r] * ghost[2 * j + r][e]
                    delta.append(value)
            deltas.append(delta)
        for i in range(4):
            for r in range(2):
                n = 2 * i + r
                cur[k + 1, i, r, :, 0:half] += jnp.where(tile_lane == 0, deltas[0][n], 0.0)
                cur[k + 1, i, r, :, half:na] += jnp.where(tile_lane == half - 1, deltas[1][n], 0.0)
        put_edges(k + 1)
        for copy in phi_copies(k + 1) + rad_copies(k + 1):
            copy.start()
        return carry

    lax.fori_loop(0, SWEEPS, sweep, 0)
    store = pltpu.make_async_copy(cur.at[SWEEPS], iterate_out, local_sem.at[0])
    store.start()
    for copy in eta_copies:
        copy.wait_send()

    own = ceta[...]
    c_below = jnp.where(has_below, ceta_rad[0], 0.0)
    c_above = jnp.where(has_above, ceta_rad[1], 0.0)
    c_left = jnp.where(has_left, eta_phi[0, 2:3, 0:half], 0.0)
    c_right = jnp.where(has_right, eta_phi[1, 2:3, 0:half], 0.0)
    faces = [
        0.5 * (own + c_below), 0.5 * (own + c_above),
        0.5 * (own + shift(own, 0, False, c_left)), 0.5 * (own + shift(own, 0, True, c_right)),
        0.5 * (own + shift(own, 1, False, own)), 0.5 * (own + shift(own, 1, True, own)),
    ]
    for n, face in enumerate(faces):
        cfaces[n] = face
    faces_sum = (faces[0] + faces[1]) + (faces[2] + faces[3]) + (faces[4] + faces[5])
    cdia[0] = faces_sum
    cdia[1] = OMEGA / (0.25 * faces_sum)
    cdia[2] = OMEGA / (0.25 * (6.0 / own))
    cdia[3] = 1.0 / own

    res = residual(SWEEPS)
    summed = jnp.concatenate([res[c][0] + res[c][1] for c in range(4)], axis=0)
    fold[0] = exact_dot(summed, pairs)
    base = fold_rows(0, 4 * (width // 2))
    sent(SWEEPS)
    ghost = columns_of(interpolate(received(SWEEPS), 0))
    tops = []
    for e in range(2):
        sign = 0.5 if e == 0 else -0.5
        terms = [jnp.zeros((width, half), F32) for _ in range(4)]
        for r in range(2):
            g = [ghost[2 * j + r][e] for j in range(4)]
            for c in range(3):
                terms[c] = terms[c] + edge_w[e, r] * g[c]
            terms[2] = terms[2] + sign * g[3]
            terms[3] = terms[3] + (edge_ie[e, r] * g[3] - sign * g[2])
        fold[1 + e] = jnp.concatenate(terms, axis=0)
        tops.append(fold_rows(1 + e, 4 * (width // 2)))
    lanes = iota(base.shape, 1)
    coarse = base + jnp.where(lanes == 0, tops[0], 0.0) + jnp.where(lanes == half - 1, tops[1], 0.0)
    coarse = (0.125 * coarse).reshape(4, width // 2, half)
    for c in range(4):
        first[c] = coarse[c] * cdia[1 if c < 3 else 2]
    for c in range(4):
        first_phi_send[0, c, :] = first[c, width // 2 - 1, :]
        first_phi_send[1, c, :] = first[c, 0, :]
    for copy in first_copies:
        copy.start()
    one = [first[c] for c in range(4)]
    lat_lo = [shift(one[c], 1, False, 0.0) for c in range(4)]
    lat_hi = [shift(one[c], 1, True, 0.0) for c in range(4)]
    arrived(first_phi, FIRST_PHI)
    arrived(first_rad, FIRST_RAD)
    low, high = [], []
    low.append([jnp.where(has_below, first_rad[0, c], 0.0) for c in range(4)])
    high.append([jnp.where(has_above, first_rad[1, c], 0.0) for c in range(4)])
    low.append([shift(one[c], 0, False, jnp.where(has_left, first_phi[0, c : c + 1, :], 0.0)) for c in range(4)])
    high.append([shift(one[c], 0, True, jnp.where(has_right, first_phi[1, c : c + 1, :], 0.0)) for c in range(4)])
    low.append(lat_lo)
    high.append(lat_hi)
    pressure = 6.0 * one[3]
    flow = jnp.zeros_like(pressure)
    for d in range(3):
        pressure = pressure - low[d][3] - high[d][3]
        flow = flow + (high[d][d] - low[d][d])
    for c in range(3):
        friction = cdia[0] * one[c]
        for d in range(3):
            friction = friction - cfaces[2 * d] * low[d][c] - cfaces[2 * d + 1] * high[d][c]
        applied = 0.25 * friction + 0.25 * (high[c][3] - low[c][3])
        coarse_out[c] = one[c] + cdia[1] * (coarse[c] - applied)
    applied = 0.25 * pressure * cdia[3] - 0.25 * flow
    coarse_out[3] = one[3] + cdia[2] * (coarse[3] - applied)
    for copy in first_copies:
        copy.wait_send()
    store.wait()


def write_out(iterate, coarse, iterate_out, coarse_out, sem):
    copies = [
        pltpu.make_async_copy(iterate, iterate_out, sem.at[0]),
        pltpu.make_async_copy(coarse, coarse_out, sem.at[1]),
    ]
    for copy in copies:
        copy.start()
    for copy in copies:
        copy.wait()


def shards(strips, layers, iterate_in, forcing, viscosity, vanka_inverse, pack_cells, take_slot, take_weight):
    _, comps, radial, width, na = iterate_in.shape
    half = na // 2
    field = (comps, radial, width, na)
    slots = WIN * CAP
    rounds = SWEEPS + 1

    def vmem(*shape, dtype=F32):
        return pltpu.VMEM(shape, dtype)

    scratch = [
        vmem(rounds, *field), vmem(*field), vmem(radial, width, na), vmem(4, *field),
        vmem(CAP, strips, dtype=jnp.int32), vmem(4, 2 * width, dtype=jnp.int32), vmem(4, 2 * width),
        vmem(na, slots, dtype=jnp.bfloat16), vmem(width, slots), vmem(2, width, slots),
        vmem(2, 4, 8, slots, dtype=jnp.int32), vmem(2, 4, 8, slots), vmem(4, 8, slots),
        vmem(radial, width, na), vmem(2, radial, width, na), vmem(2, radial, width, na), vmem(3, width, na),
        vmem(radial, width, na), vmem(2, 4, 4, radial, width, half), vmem(2, radial, width, half),
        vmem(2, radial, width, half),
        vmem(rounds, WIN, 128), vmem(rounds, WIN, 128), vmem(rounds, 2, comps, width, na),
        vmem(rounds, 2, 2 * comps, na), vmem(rounds, 2, 2 * comps, na),
        vmem(2, width, na), vmem(2, 8, na), vmem(2, 8, na), vmem(width // 2, half), vmem(2, width // 2, half),
        vmem(4, width // 2, half), vmem(6, width // 2, half),
        vmem(comps, width // 2, half), vmem(2, comps, width // 2, half), vmem(2, comps, half), vmem(2, comps, half),
        vmem(3, comps * width, half),
        pltpu.SemaphoreType.DMA((11,)), pltpu.SemaphoreType.DMA((30,)), pltpu.SemaphoreType.DMA((30,)),
    ]
    anywhere = pl.BlockSpec(memory_space=pl.ANY)
    whole = pl.BlockSpec(memory_space=pltpu.HBM)
    iterate, coarse = pl.pallas_call(
        functools.partial(kernel, strips, layers),
        out_shape=(
            pltpu.VMEM(field, F32),
            pltpu.VMEM((comps, width // 2, half), F32),
        ),
        in_specs=[whole] * 7,
        out_specs=(pl.BlockSpec(memory_space=pltpu.VMEM),) * 2,
        scratch_shapes=scratch,
        compiler_params=pltpu.CompilerParams(
            collective_id=0, has_side_effects=True, vmem_limit_bytes=60 * 1024 * 1024
        ),
        cost_estimate=pl.CostEstimate(flops=8_000_000, bytes_accessed=1_000_000, transcendentals=0),
    )(
        iterate_in[0], forcing[0], viscosity[0], vanka_inverse[0],
        pack_cells[0, 0].T, take_slot[0, 0].T, take_weight[0, 0].T,
    )
    iterate, coarse = pl.pallas_call(
        write_out,
        out_shape=(
            jax.ShapeDtypeStruct(field, F32),
            jax.ShapeDtypeStruct((comps, width // 2, half), F32),
        ),
        in_specs=[pl.BlockSpec(memory_space=pltpu.VMEM)] * 2,
        out_specs=(whole, whole),
        scratch_shapes=[pltpu.SemaphoreType.DMA((2,))],
    )(*(pltpu.with_memory_space_constraint(x, pltpu.VMEM) for x in (iterate, coarse)))
    return iterate[None], coarse[None, :, None]


def solution(mesh):
    in_specs = (
        P("patch", None, "rad", "lat", None),
        P("patch", None, "rad", "lat", None),
        P("patch", "rad", "lat", None),
        P("patch", None, None, "rad", "lat", None),
        P("patch", "lat", None, None),
        P("patch", "lat", None, None),
        P("patch", "lat", None, None),
    )
    out_specs = (P("patch", None, "rad", "lat", None), P("patch", None, "rad", "lat", None))
    part = functools.partial(shards, mesh.shape["lat"], mesh.shape["rad"])
    return jax.shard_map(part, mesh=mesh, in_specs=in_specs, out_specs=out_specs, check_vma=False)
```

```python
import functools

import jax
import jax.numpy as jnp
from jax import lax
from jax.experimental import pallas as pl
from jax.experimental.pallas import tpu as pltpu
from jax.sharding import PartitionSpec as P

SWEEPS = 3
OMEGA = 0.8
WIN = 32
CAP = 4
RIM, RAD, PHI, ETA_RAD, COARSE_RAD, ETA_PHI, FIRST_RAD, FIRST_PHI = 0, 4, 12, 20, 22, 24, 26, 28
F32 = jnp.float32


def exact_dot(values, zero_one):
    high = values.astype(jnp.bfloat16)
    rest = values - high.astype(F32)
    middle = rest.astype(jnp.bfloat16)
    low = (rest - middle.astype(F32)).astype(jnp.bfloat16)
    dot = functools.partial(jnp.dot, preferred_element_type=F32)
    return dot(high, zero_one) + (dot(middle, zero_one) + dot(low, zero_one))


def kernel(
    strips, layers,
    iterate_hbm, forcing_hbm, eta_hbm, inverse_hbm, cells_hbm, slots_hbm, weights_hbm,
    iterate_out, coarse_out,
    cur, frc, eta, vin, cel, slt, wgt,
    onehot, pick, pick_edge, take_at, take_by, slot_gain, diag, w_phi, w_lat, w_rad, inv_eta, gain, edge_w, edge_ie, edge_gain,
    rim_send, rim_recv, rad_recv, phi_send, phi_recv,
    eta_rad, eta_phi_send, eta_phi, ceta, ceta_rad, cdia, cfaces,
    first, first_rad, first_phi_send, first_phi, fold,
    local_sem, send_sem, recv_sem,
):
    patch, lat, rad = lax.axis_index("patch"), lax.axis_index("lat"), lax.axis_index("rad")
    _, _, width, na = frc.shape
    half = na // 2
    has_below, has_above = rad > 0, rad < layers - 1
    has_left, has_right = lat > 0, lat < strips - 1

    def neighbour(has, lat_step, rad_step):
        return (
            jnp.where(has, patch, 1 - patch),
            jnp.where(has, lat + lat_step, lat),
            jnp.where(has, rad + rad_step, rad),
        )

    below, above = neighbour(has_below, 0, -1), neighbour(has_above, 0, 1)
    left, right = neighbour(has_left, -1, 0), neighbour(has_right, 1, 0)
    at_above, at_right = jnp.where(has_above, 0, 1), jnp.where(has_right, 0, 1)
    at_below, at_left = jnp.where(has_below, 1, 0), jnp.where(has_left, 1, 0)

    def across(offset):
        return (1 - patch, lax.rem(lat + offset + strips, strips), rad)

    loads = [
        pltpu.make_async_copy(iterate_hbm, cur.at[0], local_sem.at[0]),
        pltpu.make_async_copy(cells_hbm, cel, local_sem.at[1]),
        pltpu.make_async_copy(eta_hbm, eta, local_sem.at[2]),
        pltpu.make_async_copy(slots_hbm, slt, local_sem.at[3]),
        pltpu.make_async_copy(weights_hbm, wgt, local_sem.at[4]),
        pltpu.make_async_copy(forcing_hbm, frc, local_sem.at[5]),
    ]
    for i in range(4):
        loads.append(
            pltpu.make_async_copy(
                inverse_hbm.at[i, pl.ds(i, 4 - i)], vin.at[i, pl.ds(i, 4 - i)], local_sem.at[6 + i]
            )
        )
    for load in loads:
        load.start()

    barrier = pltpu.get_barrier_semaphore()

    def greet(device):
        pl.semaphore_signal(barrier, inc=1, device_id=device, device_id_type=pl.DeviceIdType.MESH)

    for offset in sorted(range(-WIN // 2, WIN // 2), key=lambda o: -abs(o)):
        greet(across(offset))
    for device in (below, above, left, right):
        greet(device)

    def remote(src, dst, sem, device, landing=None):
        return pltpu.make_async_remote_copy(
            src_ref=src, dst_ref=dst, send_sem=send_sem.at[sem],
            recv_sem=recv_sem.at[sem if landing is None else landing],
            device_id=device, device_id_type=pl.DeviceIdType.MESH,
        )

    def pair(src_up, src_down, dst, sem, up, down, at_up, at_down):
        return [
            remote(src_up, dst.at[at_up], sem, up, sem + at_up),
            remote(src_down, dst.at[at_down], sem + 1, down, sem + at_down),
        ]

    def rad_pair(src_up, src_down, dst, sem):
        return pair(src_up, src_down, dst, sem, above, below, at_above, at_below)

    def phi_pair(src, dst, sem):
        return pair(src.at[0], src.at[1], dst, sem, right, left, at_right, at_left)

    def arrived(dst, sem):
        for side in range(2):
            pltpu.make_async_copy(dst.at[side], dst.at[side], recv_sem.at[sem + side]).wait()

    def rad_copies(k):
        return rad_pair(cur.at[k, :, 1], cur.at[k, :, 0], rad_recv.at[k], RAD + 2 * k)

    def phi_copies(k):
        return phi_pair(phi_send.at[k], phi_recv.at[k], PHI + 2 * k)

    def rim_start(k):
        for slot in sorted(range(WIN), key=lambda s: -abs(s - WIN // 2 + 1)):
            remote(
                rim_send.at[k, pl.ds(slot, 1)], rim_recv.at[k, pl.ds(WIN - 1 - slot, 1)], RIM + k,
                across(slot - WIN // 2 + 1),
            ).start()

    def rim_all(k, sem):
        return pltpu.make_async_copy(rim_recv.at[k], rim_recv.at[k], sem.at[RIM + k])

    eta_copies = (
        rad_pair(eta.at[1], eta.at[0], eta_rad, ETA_RAD)
        + rad_pair(ceta, ceta, ceta_rad, COARSE_RAD)
        + phi_pair(eta_phi_send, eta_phi, ETA_PHI)
    )
    first_copies = phi_pair(first_phi_send, first_phi, FIRST_PHI) + rad_pair(first, first, first_rad, FIRST_RAD)

    def iota(shape, dim):
        return lax.broadcasted_iota(jnp.int32, shape, dim)

    lane, row = iota((width, na), 1), iota((width, na), 0)
    tile_lane = iota((width, half), 1)
    slot_lane = iota((8, WIN * CAP), 1)

    def shift(x, dim, up, fill):
        count = x.shape[dim]
        at = iota(x.shape, dim)
        rolled = pltpu.roll(x, count - 1 if up else 1, dim)
        return jnp.where(at == (count - 1 if up else 0), fill, rolled)

    def put_rim(k, packed):
        tall = jnp.concatenate([jnp.where(slot_lane // WIN == s, packed, 0.0) for s in range(CAP)], axis=0)
        turned = tall.T
        rows = turned[0:WIN]
        for s in range(1, CAP):
            rows = rows + turned[s * WIN : (s + 1) * WIN]
        rim_send[k, :, 0 : 8 * CAP] = rows

    def pack(field):
        found = exact_dot(field, onehot[...]).reshape(8, width, WIN * CAP)
        return jnp.sum(found * pick[...][None], axis=1)

    def put_edges(k):
        for c in range(4):
            for r in range(2):
                phi_send[k, 0, 2 * c + r, :] = cur[k, c, r, width - 1, :]
                phi_send[k, 1, 2 * c + r, :] = cur[k, c, r, 0, :]

    def take(x, index):
        return jnp.take_along_axis(x, index, axis=1, mode="promise_in_bounds")

    pairs = (iota((na, half), 0) // 2 == iota((na, half), 1)).astype(F32).astype(jnp.bfloat16)

    def fold_rows(count):
        return fold[pl.ds(0, count, stride=2), :] + fold[pl.ds(1, count, stride=2), :]

    rim_send[...] = jnp.zeros_like(rim_send)
    eta_phi_send[...] = jnp.zeros_like(eta_phi_send)
    loads[1].wait()
    cells = cel[...].astype(F32)
    cells = jnp.concatenate([cells, cells], axis=1)
    spread = jnp.zeros((CAP, WIN * CAP), F32)
    begin = lat + strips - WIN // 2 + 1
    for s in range(CAP):
        here = (iota((CAP, WIN * CAP), 1) // WIN == s) & (iota((CAP, WIN * CAP), 0) == s)
        turn = lax.rem(WIN * s - begin + 4 * strips, 2 * strips)
        spread = jnp.where(here, pltpu.roll(cells, turn, 1), spread)
    cell = jnp.sum(spread, axis=0, keepdims=True).astype(jnp.int32)
    cell_lat, cell_lon = cell % na, cell // na
    onehot[...] = (iota((na, WIN * CAP), 0) == cell_lat).astype(F32).astype(jnp.bfloat16)
    in_lon = (iota((width, WIN * CAP), 0) == cell_lon).astype(F32)
    pick[...] = in_lon
    pick_edge[0] = jnp.where(cell_lat == 0, in_lon, 0.0)
    pick_edge[1] = jnp.where(cell_lat == na - 1, in_lon, 0.0)
    loads[0].wait()
    put_rim(0, pack(cur[0].reshape(8 * width, na)))
    put_edges(0)

    loads[2].wait()
    fold[0:width, :] = exact_dot(eta[0] + eta[1], pairs)
    coarse_eta = 0.125 * fold_rows(width // 2)
    ceta[...] = coarse_eta
    for r in range(2):
        eta_phi_send[0, r, :] = eta[r, width - 1, :]
        eta_phi_send[1, r, :] = eta[r, 0, :]
    eta_phi_send[0, 2, 0:half] = ceta[width // 2 - 1, :]
    eta_phi_send[1, 2, 0:half] = ceta[0, :]

    for load in loads[3:]:
        load.wait()
    slot = slt[...]
    strip = lax.rem(slot // CAP - lat + WIN // 2 + 2 * strips, strips)
    at = ((slot % CAP) * WIN + strip).astype(F32)
    idle = jnp.zeros((4, WIN * CAP - 2 * width), F32)
    at, by = jnp.concatenate([at, idle], axis=1), jnp.concatenate([wgt[...], idle], axis=1)
    table = jnp.concatenate([at, by], axis=0)
    beside_low, beside_high = cell_lat == 0, cell_lat == na - 1
    beside_at = jnp.where(beside_low, cell_lon, jnp.where(beside_high, cell_lon + width, 0))
    moved = take(table, jnp.broadcast_to(beside_at, (8, WIN * CAP)))
    for which, rows in ((0, table), (1, moved)):
        for n in range(4):
            take_at[which, n] = jnp.broadcast_to(rows[n : n + 1], (8, WIN * CAP)).astype(jnp.int32)
            weight = rows[4 + n : 5 + n]
            if which == 1:
                weight = jnp.where(beside_low | beside_high, weight, 0.0)
            take_by[which, n] = jnp.broadcast_to(weight, (8, WIN * CAP))

    for r in range(2):
        own = eta[r]
        lat_low = 0.5 * (own + shift(own, 1, False, own))
        lat_high = 0.5 * (own + shift(own, 1, True, own))
        inverse_eta = 1.0 / own
        w_lat[0, r], w_lat[1, r] = lat_low, lat_high
        inv_eta[r] = inverse_eta
        for e in range(2):
            at = 0 if e == 0 else na - 1

            def column(x, at=at):
                return jnp.broadcast_to(x[:, at : at + 1], (width, half))

            sign = 0.5 if e == 0 else -0.5
            w = column(lat_low if e == 0 else lat_high)
            ie = column(inverse_eta)
            edge_w[e, r], edge_ie[e, r] = w, ie
            for i in range(4):
                v = [OMEGA * column(vin[min(i, j), max(i, j), r]) for j in range(4)]
                gain[e, i, 0, r] = v[0] * w
                gain[e, i, 1, r] = v[1] * w
                gain[e, i, 2, r] = v[2] * w - sign * v[3]
                gain[e, i, 3, r] = v[3] * ie + sign * v[2]
    w_rad[1] = 0.5 * (eta[0] + eta[1])
    rows = []
    for c in range(4):
        for r in range(2):
            factors = edge_w if c < 3 else edge_ie
            low = jnp.where(tile_lane == iota((width, half), 0), factors[0, r], 0.0)
            rows.append(low + jnp.where(tile_lane == iota((width, half), 0) + width, factors[1, r], 0.0))
    edge_gain[...] = jnp.sum(jnp.stack(rows, axis=0), axis=1)
    for d in range(4):
        rows = []
        for i in range(4):
            for r in range(2):
                j = (i + d) % 4
                rows.append(gain[0, i, j, r] * pick_edge[0] + gain[1, i, j, r] * pick_edge[1])
        slot_gain[d] = jnp.sum(jnp.stack(rows, axis=0), axis=1)

    pl.semaphore_wait(barrier, WIN + 4)
    rim_start(0)
    for copy in eta_copies + phi_copies(0) + rad_copies(0):
        copy.start()

    arrived(eta_rad, ETA_RAD)
    arrived(ceta_rad, COARSE_RAD)
    arrived(eta_phi, ETA_PHI)
    eta_below = jnp.where(has_below, eta_rad[0], 0.0)
    eta_above = jnp.where(has_above, eta_rad[1], 0.0)
    w_rad[0] = 0.5 * (eta[0] + eta_below)
    w_rad[2] = 0.5 * (eta[1] + eta_above)
    for r in range(2):
        own = eta[r]
        low_row = jnp.where(has_left, eta_phi[0, r : r + 1, :], 0.0)
        high_row = jnp.where(has_right, eta_phi[1, r : r + 1, :], 0.0)
        phi_low = 0.5 * (own + shift(own, 0, False, low_row))
        phi_high = 0.5 * (own + shift(own, 0, True, high_row))
        w_phi[0, r], w_phi[1, r] = phi_low, phi_high
        diag[r] = w_rad[r] + w_rad[r + 1] + (phi_low + phi_high) + (w_lat[0, r] + w_lat[1, r])

    def residual(k):
        result = [[None, None] for _ in range(4)]
        sums = [None, None]
        flows = [None, None]
        for r in range(2):
            v = [cur[k, c, r] for c in range(4)]
            other = [cur[k, c, 1 - r] for c in range(4)]
            lo = [shift(v[c], 1, False, 0.0) for c in range(4)]
            hi = [shift(v[c], 1, True, 0.0) for c in range(4)]
            for c in range(3):
                result[c][r] = (
                    frc[c, r] - diag[r] * v[c] + w_rad[1] * other[c] + w_lat[0, r] * lo[c] + w_lat[1, r] * hi[c]
                )
            result[2][r] = result[2][r] + 0.5 * (lo[3] - hi[3])
            sums[r] = other[3] + lo[3] + hi[3] - 6.0 * v[3]
            flows[r] = hi[2] - lo[2]
            if r == 0:
                result[0][r] = result[0][r] - 0.5 * other[3]
                flows[r] = flows[r] + other[0]
            else:
                result[0][r] = result[0][r] + 0.5 * other[3]
                flows[r] = flows[r] - other[0]
        arrived(phi_recv.at[k], PHI + 2 * k)
        for r in range(2):
            lo, hi = [], []
            for c in range(4):
                v = cur[k, c, r]
                n = 2 * c + r
                lo.append(shift(v, 0, False, jnp.where(has_left, phi_recv[k, 0, n : n + 1, :], 0.0)))
                hi.append(shift(v, 0, True, jnp.where(has_right, phi_recv[k, 1, n : n + 1, :], 0.0)))
            for c in range(3):
                result[c][r] = result[c][r] + w_phi[0, r] * lo[c] + w_phi[1, r] * hi[c]
            result[1][r] = result[1][r] + 0.5 * (lo[3] - hi[3])
            sums[r] = sums[r] + lo[3] + hi[3]
            flows[r] = flows[r] + (hi[1] - lo[1])
        arrived(rad_recv.at[k], RAD + 2 * k)
        for r in range(2):
            has, sign, w = (has_below, 0.5, w_rad[0]) if r == 0 else (has_above, -0.5, w_rad[2])
            n = [jnp.where(has, rad_recv[k, r, c], 0.0) for c in range(4)]
            for c in range(3):
                result[c][r] = result[c][r] + w * n[c]
            result[0][r] = result[0][r] + sign * n[3]
            flow = flows[r] - n[0] if r == 0 else flows[r] + n[0]
            result[3][r] = frc[3, r] + inv_eta[r] * (sums[r] + n[3]) + 0.5 * flow
        return result

    def received(k):
        rim_all(k, recv_sem).wait()
        turned = jnp.concatenate([rim_recv[k]] * CAP, axis=0).T
        by_slot = turned[0:8]
        for s in range(1, CAP):
            by_slot = jnp.where(slot_lane // WIN == s, turned[8 * s : 8 * s + 8], by_slot)
        return by_slot

    def interpolate(by_slot, which):
        terms = [take_by[which, n] * take(by_slot, take_at[which, n]) for n in range(4)]
        return (terms[0] + terms[1]) + (terms[2] + terms[3])

    def columns_of(ghost):
        down = iota((8, WIN * CAP), 0)
        result = []
        for n in range(8):
            line = jnp.broadcast_to(ghost[n : n + 1], (8, WIN * CAP))
            parts = [take(line, down + 8 * m) for m in range(2 * width // 8)]
            result.append([jnp.concatenate(parts[:2], axis=0), jnp.concatenate(parts[2:], axis=0)])
        return result

    def sent(k):
        for copy in rad_copies(k) + phi_copies(k):
            copy.wait_send()
        rim_all(k, send_sem).wait()

    def sweep(k, carry):
        res = residual(k)
        scaled = [[OMEGA * res[j][r] for r in range(2)] for j in range(4)]
        for i in range(4):
            for r in range(2):
                gained = cur[k, i, r]
                for j in range(4):
                    gained = gained + vin[min(i, j), max(i, j), r] * scaled[j][r]
                cur[k + 1, i, r] = gained
        packed = pack(cur[k + 1].reshape(8 * width, na))
        sent(k)
        by_slot = received(k)
        beside = interpolate(by_slot, 1)
        for d in range(4):
            turned = beside if d == 0 else pltpu.roll(beside, 8 - 2 * d, 0)
            packed = packed + slot_gain[d] * turned
        put_rim(k + 1, packed)
        rim_start(k + 1)
        ghost = columns_of(interpolate(by_slot, 0))
        deltas = []
        for e in range(2):
            delta = []
            for i in range(4):
                for r in range(2):
                    value = gain[e, i, 0, r] * ghost[r][e]
                    for j in range(1, 4):
                        value = value + gain[e, i, j, r] * ghost[2 * j + r][e]
                    delta.append(value)
            deltas.append(delta)
        for i in range(4):
            for r in range(2):
                n = 2 * i + r
                cur[k + 1, i, r, :, 0:half] += jnp.where(tile_lane == 0, deltas[0][n], 0.0)
                cur[k + 1, i, r, :, half:na] += jnp.where(tile_lane == half - 1, deltas[1][n], 0.0)
        put_edges(k + 1)
        for copy in phi_copies(k + 1) + rad_copies(k + 1):
            copy.start()
        return carry

    lax.fori_loop(0, SWEEPS, sweep, 0)
    store = pltpu.make_async_copy(cur.at[SWEEPS], iterate_out, local_sem.at[0])
    store.start()
    for copy in eta_copies:
        copy.wait_send()

    own = ceta[...]
    c_below = jnp.where(has_below, ceta_rad[0], 0.0)
    c_above = jnp.where(has_above, ceta_rad[1], 0.0)
    c_left = jnp.where(has_left, eta_phi[0, 2:3, 0:half], 0.0)
    c_right = jnp.where(has_right, eta_phi[1, 2:3, 0:half], 0.0)
    faces = [
        0.5 * (own + c_below), 0.5 * (own + c_above),
        0.5 * (own + shift(own, 0, False, c_left)), 0.5 * (own + shift(own, 0, True, c_right)),
        0.5 * (own + shift(own, 1, False, own)), 0.5 * (own + shift(own, 1, True, own)),
    ]
    for n, face in enumerate(faces):
        cfaces[n] = face
    faces_sum = (faces[0] + faces[1]) + (faces[2] + faces[3]) + (faces[4] + faces[5])
    cdia[0] = faces_sum
    cdia[1] = OMEGA / (0.25 * faces_sum)
    cdia[2] = OMEGA / (0.25 * (6.0 / own))
    cdia[3] = 1.0 / own

    res = residual(SWEEPS)
    summed = jnp.concatenate([res[c][0] + res[c][1] for c in range(4)], axis=0)
    fold[0 : 4 * width, :] = exact_dot(summed, pairs)
    base = fold_rows(4 * (width // 2))
    sent(SWEEPS)
    ghost = interpolate(received(SWEEPS), 0)
    sign = jnp.where(slot_lane < width, 0.5, -0.5)
    component = iota(ghost.shape, 0) // 2
    added = edge_gain[...] * ghost
    added = added + jnp.where(component == 2, sign * pltpu.roll(ghost, 6, 0), 0.0)
    added = added - jnp.where(component == 3, sign * pltpu.roll(ghost, 2, 0), 0.0)
    added = added + pltpu.roll(added, 7, 0)
    down = 2 * iota((width // 2, half), 0)
    lanes = iota((width // 2, half), 1)
    coarse = []
    for c in range(4):
        line = jnp.broadcast_to(added[2 * c : 2 * c + 1], (width // 2, half))
        low, high = (take(line, down + e * width) + take(line, down + (e * width + 1)) for e in range(2))
        total = base[c * (width // 2) : (c + 1) * (width // 2)]
        total = total + jnp.where(lanes == 0, low, 0.0) + jnp.where(lanes == half - 1, high, 0.0)
        coarse.append(0.125 * total)
    for c in range(4):
        first[c] = coarse[c] * cdia[1 if c < 3 else 2]
    for c in range(4):
        first_phi_send[0, c, :] = first[c, width // 2 - 1, :]
        first_phi_send[1, c, :] = first[c, 0, :]
    for copy in first_copies:
        copy.start()
    one = [first[c] for c in range(4)]
    lat_lo = [shift(one[c], 1, False, 0.0) for c in range(4)]
    lat_hi = [shift(one[c], 1, True, 0.0) for c in range(4)]
    arrived(first_phi, FIRST_PHI)
    arrived(first_rad, FIRST_RAD)
    low, high = [], []
    low.append([jnp.where(has_below, first_rad[0, c], 0.0) for c in range(4)])
    high.append([jnp.where(has_above, first_rad[1, c], 0.0) for c in range(4)])
    low.append([shift(one[c], 0, False, jnp.where(has_left, first_phi[0, c : c + 1, :], 0.0)) for c in range(4)])
    high.append([shift(one[c], 0, True, jnp.where(has_right, first_phi[1, c : c + 1, :], 0.0)) for c in range(4)])
    low.append(lat_lo)
    high.append(lat_hi)
    pressure = 6.0 * one[3]
    flow = jnp.zeros_like(pressure)
    for d in range(3):
        pressure = pressure - low[d][3] - high[d][3]
        flow = flow + (high[d][d] - low[d][d])
    for c in range(3):
        friction = cdia[0] * one[c]
        for d in range(3):
            friction = friction - cfaces[2 * d] * low[d][c] - cfaces[2 * d + 1] * high[d][c]
        applied = 0.25 * friction + 0.25 * (high[c][3] - low[c][3])
        coarse_out[c] = one[c] + cdia[1] * (coarse[c] - applied)
    applied = 0.25 * pressure * cdia[3] - 0.25 * flow
    coarse_out[3] = one[3] + cdia[2] * (coarse[3] - applied)
    for copy in first_copies:
        copy.wait_send()
    store.wait()


def write_out(iterate, coarse, iterate_out, coarse_out, sem):
    copies = [
        pltpu.make_async_copy(iterate, iterate_out, sem.at[0]),
        pltpu.make_async_copy(coarse, coarse_out, sem.at[1]),
    ]
    for copy in copies:
        copy.start()
    for copy in copies:
        copy.wait()


def shards(strips, layers, iterate_in, forcing, viscosity, vanka_inverse, pack_cells, take_slot, take_weight):
    _, comps, radial, width, na = iterate_in.shape
    half = na // 2
    field = (comps, radial, width, na)
    slots = WIN * CAP
    rounds = SWEEPS + 1

    def vmem(*shape, dtype=F32):
        return pltpu.VMEM(shape, dtype)

    scratch = [
        vmem(rounds, *field), vmem(*field), vmem(radial, width, na), vmem(4, *field),
        vmem(CAP, strips, dtype=jnp.int32), vmem(4, 2 * width, dtype=jnp.int32), vmem(4, 2 * width),
        vmem(na, slots, dtype=jnp.bfloat16), vmem(width, slots), vmem(2, width, slots),
        vmem(2, 4, 8, slots, dtype=jnp.int32), vmem(2, 4, 8, slots), vmem(4, 8, slots),
        vmem(radial, width, na), vmem(2, radial, width, na), vmem(2, radial, width, na), vmem(3, width, na),
        vmem(radial, width, na), vmem(2, 4, 4, radial, width, half), vmem(2, radial, width, half),
        vmem(2, radial, width, half), vmem(8, slots),
        vmem(rounds, WIN, 128), vmem(rounds, WIN, 128), vmem(rounds, 2, comps, width, na),
        vmem(rounds, 2, 2 * comps, na), vmem(rounds, 2, 2 * comps, na),
        vmem(2, width, na), vmem(2, 8, na), vmem(2, 8, na), vmem(width // 2, half), vmem(2, width // 2, half),
        vmem(4, width // 2, half), vmem(6, width // 2, half),
        vmem(comps, width // 2, half), vmem(2, comps, width // 2, half), vmem(2, comps, half), vmem(2, comps, half),
        vmem(comps * width + 8, half),
        pltpu.SemaphoreType.DMA((11,)), pltpu.SemaphoreType.DMA((30,)), pltpu.SemaphoreType.DMA((30,)),
    ]
    anywhere = pl.BlockSpec(memory_space=pl.ANY)
    whole = pl.BlockSpec(memory_space=pltpu.HBM)
    iterate, coarse = pl.pallas_call(
        functools.partial(kernel, strips, layers),
        out_shape=(
            pltpu.VMEM(field, F32),
            pltpu.VMEM((comps, width // 2, half), F32),
        ),
        in_specs=[whole] * 7,
        out_specs=(pl.BlockSpec(memory_space=pltpu.VMEM),) * 2,
        scratch_shapes=scratch,
        compiler_params=pltpu.CompilerParams(
            collective_id=0, has_side_effects=True, vmem_limit_bytes=60 * 1024 * 1024
        ),
        cost_estimate=pl.CostEstimate(flops=8_000_000, bytes_accessed=1_000_000, transcendentals=0),
    )(
        iterate_in[0], forcing[0], viscosity[0], vanka_inverse[0],
        pack_cells[0, 0].T, take_slot[0, 0].T, take_weight[0, 0].T,
    )
    iterate, coarse = pl.pallas_call(
        write_out,
        out_shape=(
            jax.ShapeDtypeStruct(field, F32),
            jax.ShapeDtypeStruct((comps, width // 2, half), F32),
        ),
        in_specs=[pl.BlockSpec(memory_space=pltpu.VMEM)] * 2,
        out_specs=(whole, whole),
        scratch_shapes=[pltpu.SemaphoreType.DMA((2,))],
    )(*(pltpu.with_memory_space_constraint(x, pltpu.VMEM) for x in (iterate, coarse)))
    return iterate[None], coarse[None, :, None]


def solution(mesh):
    in_specs = (
        P("patch", None, "rad", "lat", None),
        P("patch", None, "rad", "lat", None),
        P("patch", "rad", "lat", None),
        P("patch", None, None, "rad", "lat", None),
        P("patch", "lat", None, None),
        P("patch", "lat", None, None),
        P("patch", "lat", None, None),
    )
    out_specs = (P("patch", None, "rad", "lat", None), P("patch", None, "rad", "lat", None))
    part = functools.partial(shards, mesh.shape["lat"], mesh.shape["rad"])
    return jax.shard_map(part, mesh=mesh, in_specs=in_specs, out_specs=out_specs, check_vma=False)
```
